256 devices in a mesh: dp: 2 (over core), wide: 128 (over z, x, y).
Axes of the slice: x: 4, y: 4, z: 8, core: 2. Of those that a mesh axis runs over, the one named last changes fastest.
Arguments:
- spec_cot: bfloat16 [2, 256, 256, 296], P('dp', 'wide'), may hold values from -24 to 24
- grid_state: bfloat16 [2, 512, 1024, 148], P('dp', 'wide'), may hold values from -6 to 6
- weight_in: bfloat16 [148, 256], replicated, may hold values from -0.5 to 0.5
- bias_in: float32 [256], replicated, may hold values from -4 to 4
- weight_out: bfloat16 [256, 148], replicated, may hold values from -0.375 to 0.375
- legendre: bfloat16 [256, 256, 512], P('wide'), as said below
- row_order: int32 [512], replicated, may hold values from 0 to 511, as said below
- mode_order: int32 [256], replicated, may hold values from 0 to 255, as said below
Outputs:
- spec_grad: bfloat16 [2, 256, 256, 296], P('dp', 'wide')
- grad_weight_in: float32 [148, 256], replicated
- grad_bias_in: float32 [256], replicated
- grad_weight_out: float32 [256, 148], replicated
The draws below stay inside these ranges and needn't reach their ends.
Inputs may be any that keep to these rules, and one draw needn't show every extreme that they name: `row_order`: slot 2i holds a row j with j < 256 and slot 2i + 1 its mirror row 511 - j; every row appears once. `mode_order`: slots 2i and 2i + 1 hold wavenumbers m < 128 and 255 - m; every wavenumber appears once. legendre[k, l, r] is the associated Legendre function of degree l and order mode_order[k], normalized to unit square integral over [-1, 1] without the Condon-Shortley phase, at x = cos(theta) of the row row_order[r] (theta as in the first step, x negative on the southern rows), zero for l below the order; mirror rows differ exactly by the sign (-1)^(l + m).
All inputs are finite; a program needn't handle non-finite values.
Results may differ from the reference program's by a relative error of at most 0.011.
Values may be sent and summed in bfloat16 or wider, within the bound.
A program may use at most 64 MiB of HBM per device.

```python
import math
import jax
import jax.numpy as jnp
from jax import lax

NLAT = 512
NLON = 1024
MODES = 256
HID = 256
CH = 148
SAMPLES = 2


def draw_orders(key):
    lat_key = jax.random.fold_in(key, 101)
    wave_key = jax.random.fold_in(key, 202)
    northern = jax.random.permutation(lat_key, NLAT // 2).astype(jnp.int32)
    row_order = jnp.stack([northern, NLAT - 1 - northern], axis=1).reshape(NLAT)
    lower_modes = jax.random.permutation(wave_key, MODES // 2).astype(jnp.int32)
    mode_order = jnp.stack([lower_modes, MODES - 1 - lower_modes], axis=1).reshape(MODES)
    return (row_order, mode_order)


def legendre_values(mode_order, row_order):
    north_index = jnp.minimum(row_order, NLAT - 1 - row_order)
    mirror_sign = jnp.where(row_order == north_index, 1.0, -1.0)
    colatitude = (north_index.astype(jnp.float32) + 0.5) * (math.pi / NLAT)
    cosine_vals = (mirror_sign * jnp.cos(colatitude))[None, :]
    sine_vals = jnp.sin(colatitude)[None, :]
    order_real = mode_order.astype(jnp.float32)[:, None]
    order_col = mode_order[:, None]
    half_gamma = 0.5 * math.log(math.pi) - math.log(2.0)
    log_start = 0.5 * (jax.scipy.special.gammaln(order_real + 1.5) - jax.scipy.special.gammaln(order_real + 1.0) - half_gamma) - 0.5 * math.log(2.0) + order_real * jnp.log(sine_vals)
    zero_state = jnp.zeros((MODES, NLAT), jnp.float32)

    def recur(state_carry, degree):
        prev_one, prev_two, log_scale = state_carry
        degree_real = degree.astype(jnp.float32)
        denom_first = jnp.maximum(degree_real * degree_real - order_real * order_real, 1.0)
        recur_first = jnp.sqrt((4.0 * degree_real * degree_real - 1.0) / denom_first)
        denom_second = jnp.maximum(4.0 * (degree_real - 1.0) * (degree_real - 1.0) - 1.0, 1.0)
        recur_second = jnp.sqrt(jnp.maximum((degree_real - 1.0) * (degree_real - 1.0) - order_real * order_real, 0.0) / denom_second)
        general = recur_first * (cosine_vals * prev_one - recur_second * prev_two)
        second = jnp.sqrt(2.0 * order_real + 3.0) * cosine_vals * prev_one
        current = jnp.where(degree == order_col, 1.0, jnp.where(degree == order_col + 1, second, jnp.where(degree > order_col + 1, general, 0.0)))
        too_large = jnp.abs(current) > 1000000000000.0
        factor = jnp.where(too_large, 2.0 ** (-40), 1.0)
        result = current * jnp.exp(log_scale)
        new_carry = (current * factor, prev_one * factor, log_scale + jnp.where(too_large, 40.0 * math.log(2.0), 0.0))
        return (new_carry, result)
    degrees = jnp.arange(MODES, dtype=jnp.int32)
    unused, stacked = lax.scan(recur, (zero_state, zero_state, log_start), degrees)
    return jnp.transpose(stacked, (1, 0, 2))


def draw_row_order(key, part):
    row_order, mode_order = draw_orders(key)
    return row_order


def draw_mode_order(key, part):
    row_order, mode_order = draw_orders(key)
    return mode_order


def draw_legendre(key, part):
    row_order, mode_order = draw_orders(key)
    return legendre_values(mode_order, row_order).astype(jnp.bfloat16)


def block_levels(stream_key, extent, split, low, high):
    loudness, own = 1.0, jax.random.fold_in(stream_key, 6)
    for axis_at, blocks in split:
        steps = jnp.exp(jax.random.uniform(jax.random.fold_in(own, axis_at), (blocks,), jnp.float32, low / len(split), high / len(split)))
        loudness = loudness * jnp.repeat(steps, extent[axis_at] // blocks).reshape([-1 if axis == axis_at else 1 for axis in range(len(extent))])
    return loudness


def noise(own_key, shape, width, limit, cuts=(), kind=jnp.bfloat16):
    drawn = width * jax.random.normal(own_key, shape, jnp.float32)
    if cuts:
        drawn = drawn * block_levels(own_key, shape, cuts, -0.22, 0.18)
    return jnp.clip(drawn, -limit, limit).astype(kind)


def setup_inputs(seed: int = 0) -> dict:
    arg_keys = jax.random.split(jax.random.key(seed), 9)
    return {
        "spec_cot": noise(arg_keys[0], (SAMPLES, MODES, MODES, 2 * CH), 4.0, 24.0, ((0, 2), (1, 128))),
        "grid_state": noise(arg_keys[1], (SAMPLES, NLAT, NLON, CH), 1.0, 6.0, ((0, 2), (1, 128))),
        "weight_in": noise(arg_keys[2], (CH, HID), CH ** -0.5, 0.5),
        "bias_in": noise(arg_keys[3], (HID,), 1.0, 4.0, (), jnp.float32),
        "weight_out": noise(arg_keys[4], (HID, CH), HID ** -0.5, 0.375),
        "legendre": draw_legendre(jax.random.fold_in(arg_keys[8], 71), 0),
        "row_order": draw_row_order(jax.random.fold_in(arg_keys[8], 71), 0),
        "mode_order": draw_mode_order(jax.random.fold_in(arg_keys[8], 71), 0),
    }


def row_weights(row_order, lat_total):
    north_index = jnp.minimum(row_order, lat_total - 1 - row_order)
    colatitude = (north_index.astype(jnp.float32) + 0.5) * (math.pi / lat_total)
    return jnp.sin(colatitude) * (math.pi / lat_total)


def wave_angles(mode_order, lon_total):
    longitude = jnp.arange(lon_total, dtype=jnp.int32)
    phase_index = (mode_order[:, None] * longitude[None, :]) % lon_total
    return phase_index.astype(jnp.float32) * (2.0 * math.pi / lon_total)


def back_table(mode_order, lon_total):
    angles = wave_angles(mode_order, lon_total)
    return jnp.stack([jnp.cos(angles) / lon_total, -jnp.sin(angles) / lon_total], axis=1).astype(jnp.bfloat16)


def forward_table(mode_order, lon_total):
    angles = wave_angles(mode_order, lon_total)
    multiple = jnp.where(mode_order == 0, 1.0, 2.0)[:, None]
    stacked = jnp.stack([multiple * jnp.cos(angles), -multiple * jnp.sin(angles)], axis=2)
    return jnp.transpose(stacked, (1, 0, 2)).astype(jnp.bfloat16)


def reference(spec_cot, grid_state, weight_in, bias_in, weight_out, legendre, row_order, mode_order):
    samples = grid_state.shape[0]
    lat_total = grid_state.shape[1]
    lon_total = grid_state.shape[2]
    channels = grid_state.shape[3]
    hidden = weight_in.shape[1]
    weights = row_weights(row_order, lat_total)
    basis = legendre.astype(jnp.float32)
    summed = jnp.einsum("kla,sklc->sakc", basis, spec_cot.astype(jnp.float32))
    fourier_cot = (summed * weights[None, :, None, None]).astype(jnp.bfloat16)
    cot_parts = fourier_cot.reshape(samples, lat_total, -1, 2, channels)
    grid_cot = jnp.einsum("sakpc,kpl->salc", cot_parts.astype(jnp.float32),
                          back_table(mode_order, lon_total).astype(jnp.float32)).astype(jnp.bfloat16)

    block_rows = min(8, lat_total)
    block_count = lat_total // block_rows

    def to_blocks(grid_field):
        return jnp.moveaxis(grid_field.reshape(samples, block_count, block_rows, lon_total, channels), 1, 0)

    def column_block(totals, pieces):
        state_block, cot_block = pieces
        state_rows = state_block.reshape(-1, channels)
        cot_rows = cot_block.reshape(-1, channels)
        preact = jnp.dot(state_rows, weight_in, preferred_element_type=jnp.float32) + bias_in
        sigmoid_pre = jax.nn.sigmoid(preact)
        activation = (preact * sigmoid_pre).astype(jnp.bfloat16)
        back_hidden = jnp.dot(cot_rows, weight_out.T, preferred_element_type=jnp.float32)
        grad_preact = (back_hidden * sigmoid_pre * (1.0 + preact * (1.0 - sigmoid_pre))).astype(jnp.bfloat16)
        dstate = jnp.dot(grad_preact, weight_in.T, preferred_element_type=jnp.float32).astype(jnp.bfloat16)
        new_totals = (totals[0] + jnp.dot(state_rows.T, grad_preact, preferred_element_type=jnp.float32),
                      totals[1] + jnp.sum(grad_preact.astype(jnp.float32), axis=0),
                      totals[2] + jnp.dot(activation.T, cot_rows, preferred_element_type=jnp.float32))
        return new_totals, dstate.reshape(state_block.shape)

    initial = (jnp.zeros((channels, hidden), jnp.float32), jnp.zeros((hidden,), jnp.float32),
               jnp.zeros((hidden, channels), jnp.float32))
    totals, dstate_blocks = lax.scan(column_block, initial, (to_blocks(grid_state), to_blocks(grid_cot)))
    dstate = jnp.moveaxis(dstate_blocks, 0, 1).reshape(samples, lat_total, lon_total, channels)
    fourier_grad = jnp.einsum("salc,lkp->sakpc", dstate.astype(jnp.float32),
                              forward_table(mode_order, lon_total).astype(jnp.float32)).astype(jnp.bfloat16)
    fourier_grad = fourier_grad.reshape(samples, lat_total, -1, 2 * channels)
    spec_grad = jnp.einsum("kla,sakc->sklc", basis, fourier_grad.astype(jnp.float32)).astype(jnp.bfloat16)
    return spec_grad, totals[0], totals[1], totals[2]
```

```python
import math

import jax
import jax.numpy as jnp
from jax import lax
from jax.sharding import PartitionSpec as P


def row_weights(row_order, lat_total):
    north_index = jnp.minimum(row_order, lat_total - 1 - row_order)
    colatitude = (north_index.astype(jnp.float32) + 0.5) * (math.pi / lat_total)
    return jnp.sin(colatitude) * (math.pi / lat_total)


def wave_angles(mode_order, lon_total):
    longitude = jnp.arange(lon_total, dtype=jnp.int32)
    phase_index = mode_order[:, None] * longitude[None, :] % lon_total
    return phase_index.astype(jnp.float32) * (2.0 * math.pi / lon_total)


def back_table(mode_order, lon_total):
    angles = wave_angles(mode_order, lon_total)
    return jnp.stack([jnp.cos(angles) / lon_total, -jnp.sin(angles) / lon_total], axis=1).astype(
        jnp.bfloat16
    )


def forward_table(mode_order, lon_total):
    angles = wave_angles(mode_order, lon_total)
    multiple = jnp.where(mode_order == 0, 1.0, 2.0)[:, None]
    stacked = jnp.stack([multiple * jnp.cos(angles), -multiple * jnp.sin(angles)], axis=2)
    return jnp.transpose(stacked, (1, 0, 2)).astype(jnp.bfloat16)


def sum_everywhere(*terms):
    shards = lax.axis_size("wide")
    flat = jnp.concatenate([term.reshape(-1) for term in terms])
    size = flat.shape[0]
    width = -(-size // (shards * 128)) * 128
    blocks = jnp.pad(flat, (0, shards * width - size)).reshape(shards, width)
    pieces = lax.all_to_all(blocks, "wide", split_axis=0, concat_axis=0, tiled=True)
    part = jnp.sum(pieces, axis=0)
    part = part + lax.ppermute(part, "dp", [(0, 1), (1, 0)])
    spread = jnp.broadcast_to(part[None], (shards, width))
    whole = lax.all_to_all(spread, "wide", split_axis=0, concat_axis=0, tiled=True).reshape(-1)
    out, start = [], 0
    for term in terms:
        out.append(whole[start : start + term.size].reshape(term.shape))
        start += term.size
    return out


def per_device(
    spec_cot, grid_state, weight_in, bias_in, weight_out, legendre, row_order, mode_order
):
    samples = grid_state.shape[0]
    lat_local = grid_state.shape[1]
    lon_total = grid_state.shape[2]
    channels = grid_state.shape[3]
    lat_total = row_order.shape[0]
    mode_total = mode_order.shape[0]
    weights = row_weights(row_order, lat_total)
    summed = jnp.einsum("kla,sklc->sakc", legendre, spec_cot, preferred_element_type=jnp.float32)
    fourier_cot = (summed * weights[None, :, None, None]).astype(jnp.bfloat16)
    fourier_rows = lax.all_to_all(fourier_cot, "wide", split_axis=1, concat_axis=2, tiled=True)
    cot_parts = fourier_rows.reshape(samples, lat_local, mode_total, 2, channels)
    grid_cot = jnp.einsum(
        "sakpc,kpl->salc",
        cot_parts,
        back_table(mode_order, lon_total),
        preferred_element_type=jnp.float32,
    ).astype(jnp.bfloat16)
    state_rows = grid_state.reshape(-1, channels)
    cot_rows = grid_cot.reshape(-1, channels)
    preact = jnp.dot(state_rows, weight_in, preferred_element_type=jnp.float32) + bias_in
    sigmoid_pre = jax.nn.sigmoid(preact)
    activation = (preact * sigmoid_pre).astype(jnp.bfloat16)
    back_hidden = jnp.einsum("rc,hc->rh", cot_rows, weight_out, preferred_element_type=jnp.float32)
    grad_preact = (back_hidden * sigmoid_pre * (1.0 + preact * (1.0 - sigmoid_pre))).astype(
        jnp.bfloat16
    )
    dstate = jnp.einsum(
        "rh,ch->rc", grad_preact, weight_in, preferred_element_type=jnp.float32
    ).astype(jnp.bfloat16)
    local_in = jnp.einsum("rc,rh->ch", state_rows, grad_preact, preferred_element_type=jnp.float32)
    local_bias = jnp.sum(grad_preact.astype(jnp.float32), axis=0)
    local_out = jnp.einsum("rh,rc->hc", activation, cot_rows, preferred_element_type=jnp.float32)
    grad_weight_in, grad_bias_in, grad_weight_out = sum_everywhere(local_in, local_bias, local_out)
    dstate_grid = dstate.reshape(samples, lat_local, lon_total, channels)
    fourier_grad = jnp.einsum(
        "salc,lkp->sakpc",
        dstate_grid,
        forward_table(mode_order, lon_total),
        preferred_element_type=jnp.float32,
    ).astype(jnp.bfloat16)
    fourier_grad = fourier_grad.reshape(samples, lat_local, mode_total, 2 * channels)
    gathered = lax.all_to_all(fourier_grad, "wide", split_axis=2, concat_axis=1, tiled=True)
    spec_grad = jnp.einsum(
        "kla,sakc->sklc", legendre, gathered, preferred_element_type=jnp.float32
    ).astype(jnp.bfloat16)
    return (spec_grad, grad_weight_in, grad_bias_in, grad_weight_out)


def solution(mesh):
    placed = (
        P("dp", "wide", None, None),
        P("dp", "wide", None, None),
        P(),
        P(),
        P(),
        P("wide", None, None),
        P(),
        P(),
    )
    return jax.shard_map(
        per_device,
        mesh=mesh,
        in_specs=placed,
        out_specs=(P("dp", "wide", None, None), P(), P(), P()),
        check_vma=False,
    )
```

```python
import functools
import math

import jax
import jax.numpy as jnp
from jax import lax
from jax.experimental import pallas as pl
from jax.experimental.pallas import tpu as pltpu
from jax.sharding import PartitionSpec as P


MESH = pl.DeviceIdType.MESH
PLANE = 16


def exchange_kernel(n, x_ref, o_ref, send_sem, recv_sem, own_sem, ready):
    me = lax.axis_index("wide")
    lines = n // PLANE
    line, spot = me // PLANE, me % PLANE

    def along(t):
        return {"wide": (line + t) % lines * PLANE + spot}

    def across(t):
        return {"wide": line * PLANE + (spot + t) % PLANE}

    barrier = pltpu.get_barrier_semaphore()

    @pl.loop(1, lines)
    def _(t):
        pl.semaphore_signal(barrier, inc=1, device_id=along(t), device_id_type=MESH)

    @pl.loop(1, PLANE)
    def _(t):
        pl.semaphore_signal(barrier, inc=1, device_id=across(t), device_id_type=MESH)

    own = pltpu.make_async_copy(x_ref.at[me], o_ref.at[me], own_sem)
    own.start()
    pl.semaphore_wait(barrier, lines + PLANE - 2)

    @pl.loop(1, PLANE)
    def _(t):
        pl.semaphore_signal(ready, inc=1, device_id=across(t), device_id_type=MESH)

    pl.semaphore_wait(ready, PLANE - 1)

    @pl.loop(1, n)
    def _(t):
        to = (line + t) % lines * PLANE + (spot + t // lines) % PLANE
        pltpu.make_async_remote_copy(
            x_ref.at[to],
            o_ref.at[me],
            send_sem,
            recv_sem,
            device_id={"wide": to},
            device_id_type=MESH,
        ).start()

    own.wait()
    rest = pltpu.make_async_remote_copy(
        x_ref.at[pl.ds(0, n - 1)],
        o_ref.at[pl.ds(0, n - 1)],
        send_sem,
        recv_sem,
        device_id=across(1),
        device_id_type=MESH,
    )
    rest.wait_send()
    rest.wait_recv()


def exchange(x, number):
    n = x.shape[0]
    return pl.pallas_call(
        functools.partial(exchange_kernel, n),
        name=f"exchange_{number}",
        out_shape=jax.ShapeDtypeStruct(x.shape, x.dtype),
        in_specs=[pl.BlockSpec(memory_space=pltpu.VMEM)],
        out_specs=pl.BlockSpec(memory_space=pltpu.VMEM),
        scratch_shapes=[
            pltpu.SemaphoreType.DMA(()),
            pltpu.SemaphoreType.DMA(()),
            pltpu.SemaphoreType.DMA(()),
            pltpu.SemaphoreType.REGULAR,
        ],
        compiler_params=pltpu.CompilerParams(
            collective_id=number, has_side_effects=True, vmem_limit_bytes=32 * 2**20
        ),
    )(x)


def row_weights(row_order, lat_total):
    north_index = jnp.minimum(row_order, lat_total - 1 - row_order)
    colatitude = (north_index.astype(jnp.float32) + 0.5) * (math.pi / lat_total)
    return jnp.sin(colatitude) * (math.pi / lat_total)


def wave_angles(mode_order, lon_total):
    longitude = jnp.arange(lon_total, dtype=jnp.int32)
    phase_index = mode_order[:, None] * longitude[None, :] % lon_total
    return phase_index.astype(jnp.float32) * (2.0 * math.pi / lon_total)


def back_table(mode_order, lon_total):
    angles = wave_angles(mode_order, lon_total)
    return jnp.stack([jnp.cos(angles) / lon_total, -jnp.sin(angles) / lon_total], axis=1).astype(
        jnp.bfloat16
    )


def forward_table(mode_order, lon_total):
    angles = wave_angles(mode_order, lon_total)
    multiple = jnp.where(mode_order == 0, 1.0, 2.0)[:, None]
    stacked = jnp.stack([multiple * jnp.cos(angles), -multiple * jnp.sin(angles)], axis=2)
    return jnp.transpose(stacked, (1, 0, 2)).astype(jnp.bfloat16)


def sum_everywhere(*terms):
    shards = lax.axis_size("wide")
    flat = jnp.concatenate([term.reshape(-1) for term in terms])
    size = flat.shape[0]
    width = -(-size // (shards * 128)) * 128
    blocks = jnp.pad(flat, (0, shards * width - size)).reshape(shards, width)
    pieces = exchange(blocks.reshape(shards, width // 128, 128), 3)
    part = jnp.sum(pieces, axis=0)
    part = part + lax.ppermute(part, "dp", [(0, 1), (1, 0)])
    spread = jnp.broadcast_to(part[None], (shards, width // 128, 128))
    whole = exchange(spread, 4).reshape(-1)
    out, start = [], 0
    for term in terms:
        out.append(whole[start : start + term.size].reshape(term.shape))
        start += term.size
    return out


def per_device(
    spec_cot, grid_state, weight_in, bias_in, weight_out, legendre, row_order, mode_order
):
    samples = grid_state.shape[0]
    lat_local = grid_state.shape[1]
    lon_total = grid_state.shape[2]
    channels = grid_state.shape[3]
    lat_total = row_order.shape[0]
    mode_total = mode_order.shape[0]
    weights = row_weights(row_order, lat_total)
    summed = jnp.einsum("kla,sklc->sakc", legendre, spec_cot, preferred_element_type=jnp.float32)
    fourier_cot = (summed * weights[None, :, None, None]).astype(jnp.bfloat16)
    shards = lat_total // lat_local
    own_modes = mode_total // shards
    packed = fourier_cot.reshape(shards, lat_local, own_modes * 2 * channels)
    packed = jnp.pad(packed, ((0, 0), (0, 0), (0, -packed.shape[2] % 128)))
    fourier_rows = exchange(packed, 1)[:, :, : own_modes * 2 * channels]
    cot_parts = jnp.swapaxes(fourier_rows, 0, 1).reshape(
        samples, lat_local, mode_total, 2, channels
    )
    grid_cot = jnp.einsum(
        "sakpc,kpl->salc",
        cot_parts,
        back_table(mode_order, lon_total),
        preferred_element_type=jnp.float32,
    ).astype(jnp.bfloat16)
    state_rows = grid_state.reshape(-1, channels)
    cot_rows = grid_cot.reshape(-1, channels)
    preact = jnp.dot(state_rows, weight_in, preferred_element_type=jnp.float32) + bias_in
    sigmoid_pre = jax.nn.sigmoid(preact)
    activation = (preact * sigmoid_pre).astype(jnp.bfloat16)
    back_hidden = jnp.einsum("rc,hc->rh", cot_rows, weight_out, preferred_element_type=jnp.float32)
    grad_preact = (back_hidden * sigmoid_pre * (1.0 + preact * (1.0 - sigmoid_pre))).astype(
        jnp.bfloat16
    )
    dstate = jnp.einsum(
        "rh,ch->rc", grad_preact, weight_in, preferred_element_type=jnp.float32
    ).astype(jnp.bfloat16)
    local_in = jnp.einsum("rc,rh->ch", state_rows, grad_preact, preferred_element_type=jnp.float32)
    local_bias = jnp.sum(grad_preact.astype(jnp.float32), axis=0)
    local_out = jnp.einsum("rh,rc->hc", activation, cot_rows, preferred_element_type=jnp.float32)
    grad_weight_in, grad_bias_in, grad_weight_out = sum_everywhere(local_in, local_bias, local_out)
    dstate_grid = dstate.reshape(samples, lat_local, lon_total, channels)
    fourier_grad = jnp.einsum(
        "salc,lkp->sakpc",
        dstate_grid,
        forward_table(mode_order, lon_total),
        preferred_element_type=jnp.float32,
    ).astype(jnp.bfloat16)
    packed = fourier_grad.reshape(lat_local, shards, own_modes * 2 * channels)
    packed = jnp.pad(jnp.swapaxes(packed, 0, 1), ((0, 0), (0, 0), (0, -packed.shape[2] % 128)))
    gathered = exchange(packed, 2)[:, :, : own_modes * 2 * channels]
    gathered = gathered.reshape(samples, lat_total, own_modes, 2 * channels)
    spec_grad = jnp.einsum(
        "kla,sakc->sklc", legendre, gathered, preferred_element_type=jnp.float32
    ).astype(jnp.bfloat16)
    return (spec_grad, grad_weight_in, grad_bias_in, grad_weight_out)


def solution(mesh):
    placed = (
        P("dp", "wide", None, None),
        P("dp", "wide", None, None),
        P(),
        P(),
        P(),
        P("wide", None, None),
        P(),
        P(),
    )
    return jax.shard_map(
        per_device,
        mesh=mesh,
        in_specs=placed,
        out_specs=(P("dp", "wide", None, None), P(), P(), P()),
        check_vma=False,
    )
```

```python
import functools
import math

import jax
import jax.numpy as jnp
from jax import lax
from jax.experimental import pallas as pl
from jax.experimental.pallas import tpu as pltpu
from jax.sharding import PartitionSpec as P

MESH = pl.DeviceIdType.MESH
F32 = jnp.float32
BF16 = jnp.bfloat16
CHUNKS = 2
LANES = 128
PLANE = 16
TURN = 2.0 * math.pi


def dot(a, b):
    return jnp.dot(a, b, preferred_element_type=F32)


def dot_nt(a, b):
    return lax.dot_general(a, b, (((1,), (1,)), ((), ())), preferred_element_type=F32)


def iota(shape, axis):
    return lax.broadcasted_iota(jnp.int32, shape, axis)


def ones_where(mask):
    return jnp.where(mask, 1.0, 0.0).astype(BF16)


def step_kernel(
    sizes,
    spec_hbm,
    state_hbm,
    win_ref,
    bias_ref,
    wout_ref,
    leg_hbm,
    rows_ref,
    modes_ref,
    spec_grad_ref,
    gin_ref,
    gbias_ref,
    gout_ref,
    spec_v,
    state_v,
    leg_v,
    legp,
    spec_pad,
    coef,
    win_ext,
    win_t,
    wout_t,
    table,
    scale_v,
    columns,
    factor,
    active,
    lhs,
    grid_cot,
    dstate,
    zbuf,
    out_acc,
    send1,
    recv1,
    send2,
    recv2,
    acc,
    part,
    pieces,
    zpieces,
    result,
    load_sem,
    a2a_send,
    a2a_recv,
    sum_send,
    sum_recv,
    ready,
):
    n, rows, chans, pad, lon, hid = sizes
    per = rows // CHUNKS
    group = per * n
    total = rows * n
    lines = n // PLANE
    me = lax.axis_index("wide")
    core = lax.axis_index("dp")
    line, spot = lax.div(me, PLANE), lax.rem(me, PLANE)
    line_at = [lax.rem(line + t, lines) * PLANE for t in range(lines)]

    def spot_at(t):
        return lax.rem(spot + t, PLANE)

    leg_copy = pltpu.make_async_copy(leg_hbm, leg_v, load_sem.at[0])
    spec_copy = pltpu.make_async_copy(spec_hbm, spec_v, load_sem.at[1])
    state_copy = pltpu.make_async_copy(state_hbm, state_v, load_sem.at[2])
    leg_copy.start()
    spec_copy.start()
    state_copy.start()

    barrier = pltpu.get_barrier_semaphore()
    for t in range(1, lines):
        pl.semaphore_signal(
            barrier, inc=1, device_id={"wide": line_at[t] + spot}, device_id_type=MESH
        )
    for t in range(1, PLANE):
        pl.semaphore_signal(
            barrier, inc=1, device_id={"wide": line_at[0] + spot_at(t)}, device_id_type=MESH
        )
    for t in range(PLANE):
        pl.semaphore_signal(
            barrier,
            inc=1,
            device_id={"dp": 1 - core, "wide": line_at[0] + spot_at(t)},
            device_id_type=MESH,
        )

    def chunked(at):
        ch = lax.div(at, group)
        inner = at - ch * group
        owner = lax.div(inner, per)
        return owner * rows + ch * per + (inner - owner * per)

    order = ones_where(iota((total, total), 0) == chunked(iota((total, total), 1)))
    row_at = rows_ref[...]
    north = jnp.minimum(row_at, total - 1 - row_at).astype(F32).astype(BF16)
    north = dot(jnp.broadcast_to(north, (16, total)), order)
    weights = jnp.sin((north[0:8] + 0.5) * (math.pi / total)) * (math.pi / total)

    modes = modes_ref[...].astype(F32).astype(BF16)
    modes = jnp.broadcast_to(modes, (LANES, 2 * n))

    leg_copy.wait()
    for i in range(2):
        legp[i] = dot(leg_v[i], order).astype(BF16)
    spec_copy.wait()
    zero_rows = jnp.zeros((pad - chans, spec_v.shape[2]), F32)
    for i in range(2):
        both = spec_v[i].astype(F32)
        spec_pad[...] = jnp.concatenate(
            [both[0:chans], zero_rows, both[chans : 2 * chans], zero_rows], axis=0
        ).astype(BF16)
        got = dot(spec_pad[...], legp[i])
        coef[pl.ds(i * 2 * pad, 2 * pad), :] = (got * weights[0:1]).astype(BF16)

    def to_messages(flat):
        return flat.reshape(n, per, 4 * pad)

    for ch in range(CHUNKS):
        send1[ch] = to_messages(coef[:, pl.ds(ch * group, group)].T)
        recv1[ch, me] = send1[ch, me]

    pl.semaphore_wait(barrier, lines - 1 + 2 * PLANE - 1)
    for t in range(1, PLANE):
        pl.semaphore_signal(
            ready, inc=1, device_id={"wide": line_at[0] + spot_at(t)}, device_id_type=MESH
        )
    pl.semaphore_wait(ready, PLANE - 1)

    def spread(src, dst, slot):
        def go(to):
            pltpu.make_async_remote_copy(
                src.at[to],
                dst.at[me],
                a2a_send.at[slot],
                a2a_recv.at[slot],
                device_id={"wide": to},
                device_id_type=MESH,
            ).start()

        for t in range(1, lines):
            go(line_at[t] + spot)

        @pl.loop(1, PLANE)
        def _(t):
            at = spot_at(t)
            for s in range(lines):
                go(line_at[s] + at)

    def spread_rest(src, dst, slot):
        return pltpu.make_async_remote_copy(
            src.at[pl.ds(0, n - 1)],
            dst.at[pl.ds(0, n - 1)],
            a2a_send.at[slot],
            a2a_recv.at[slot],
            device_id={"wide": line_at[1] + spot},
            device_id_type=MESH,
        )

    for ch in range(CHUNKS):
        spread(send1.at[ch], recv1.at[ch], ch)

    win_rows = win_ref[...].astype(F32)
    bias = bias_ref[...]
    bias_parts = []
    for _ in range(3):
        high = bias.astype(BF16).astype(F32)
        bias_parts.append(high)
        bias = bias - high
    rest_rows = jnp.zeros((pad - chans - 3, hid), F32)
    extended = jnp.concatenate([win_rows] + bias_parts + [rest_rows], axis=0)
    win_ext[...] = extended.astype(BF16)
    win_t[...] = extended.T.astype(BF16)
    wout_rows = jnp.concatenate(
        [wout_ref[...].astype(F32), jnp.zeros((pad - chans, hid), F32)], axis=0
    )
    wout_t[...] = wout_rows.T.astype(BF16)

    state_copy.wait()
    flat_state = state_v[...].reshape(chans * rows, lon)
    row_id = iota((pad, lon), 0)
    one_rows = jnp.logical_and(row_id >= chans, row_id < chans + 3)
    for j in range(rows):
        pick = ones_where(
            iota((pad, chans * rows), 1) == rows * iota((pad, chans * rows), 0) + j
        )
        columns[j] = jnp.where(one_rows, 1.0, dot(pick, flat_state)).astype(BF16)

    @pl.loop(0, rows)
    def _(j):
        preact = dot(win_t[...], columns[j])
        gate = jax.nn.sigmoid(preact)
        active[j] = (preact * gate).astype(BF16)
        factor[j] = gate * (1.0 + preact * (1.0 - gate))

    for i in range(2):
        choose = ones_where(iota((n, 2 * n), 1) == 2 * iota((n, 2 * n), 0) + i)
        mode = dot_nt(choose, modes)
        phase = mode * iota((n, LANES), 1).astype(F32)
        phase = phase - lon * jnp.floor(phase * (1.0 / lon))
        real, imag = jnp.cos(phase * (TURN / lon)), jnp.sin(phase * (TURN / lon))
        parts = lon // LANES
        jump = mode - parts * jnp.floor(mode * (1.0 / parts))
        jump_real, jump_imag = jnp.cos(jump * (TURN / parts)), jnp.sin(jump * (TURN / parts))
        for b in range(parts):
            at = pl.ds(b * LANES, LANES)
            table[pl.ds(2 * i * n, n), at] = real.astype(BF16)
            table[pl.ds((2 * i + 1) * n, n), at] = (-imag).astype(BF16)
            real, imag = real * jump_real - imag * jump_imag, imag * jump_real + real * jump_imag
    slot_modes = []
    for i in range(2):
        choose = ones_where(iota((2 * n, n), 0) == 2 * iota((2 * n, n), 1) + i)
        slot_modes += [dot(modes[0:16], choose)] * 2
    scale_v[...] = jnp.where(jnp.concatenate(slot_modes, axis=1) == 0.0, 1.0, 2.0)[0:8]

    def row_major(at):
        j = lax.div(at, n)
        return (at - j * n) * per + j

    regroup = ones_where(iota((group, group), 0) == row_major(iota((group, group), 1)))

    for ch in range(CHUNKS):
        spread_rest(send1.at[ch], recv1.at[ch], ch).wait_recv()
        arrived = recv1[ch].reshape(group, 4 * pad).T
        arrived = dot(arrived, regroup).astype(BF16)
        for j in range(per):
            for q in range(4):
                lhs[pl.ds(j * pad, pad), pl.ds(q * n, n)] = arrived[
                    q * pad : (q + 1) * pad, j * n : (j + 1) * n
                ]
        grid_cot[ch] = (dot(lhs[...], table[...]) * (1.0 / lon)).astype(BF16)
        for j in range(per):
            row = ch * per + j
            mine = pl.ds(j * pad, pad)
            cot_row = grid_cot[ch, mine, :]
            grad_preact = (dot(wout_t[...], cot_row) * factor[row]).astype(BF16)
            dstate[mine, :] = dot(win_ext[...], grad_preact).astype(BF16)
            grad_in = dot_nt(columns[row], grad_preact)
            grad_out = dot_nt(cot_row, active[row])
            if row == 0:
                acc[0] = grad_in
                acc[1] = grad_out
            else:
                acc[0] += grad_in
                acc[1] += grad_out
        back = (dot_nt(dstate[...], table[...]) * scale_v[0:1, :]).astype(BF16)
        for j in range(per):
            for q in range(4):
                zbuf[pl.ds(q * pad, pad), pl.ds(j * n, n)] = back[
                    j * pad : (j + 1) * pad, q * n : (q + 1) * n
                ]
        send2[ch] = to_messages(dot_nt(regroup, zbuf[...]).astype(BF16))
        recv2[ch, me] = send2[ch, me]
        spread(send2.at[ch], recv2.at[ch], CHUNKS + ch)

    share = 2 * pad // (2 * PLANE) // 2
    part[...] = acc[...].reshape(2, pad // 2, 2, hid)

    def piece(c, s):
        return part.at[c, pl.ds(s * share, share)]

    def meet(src, dst, slot, to):
        return pltpu.make_async_remote_copy(
            src,
            dst,
            sum_send.at[slot],
            sum_recv.at[slot],
            device_id=to,
            device_id_type=MESH,
        )

    mine = core * PLANE + spot
    pieces[mine] = part[core, pl.ds(spot * share, share)]
    for t in range(PLANE):
        for c in (1, 0):
            if t or c:
                owner = lax.rem(core + c, 2)
                at = spot_at(t)
                to = {"dp": owner, "wide": line_at[0] + at}
                meet(piece(owner, at), pieces.at[mine], 0, to).start()
    others = meet(
        pieces.at[pl.ds(0, 2 * PLANE - 1)],
        pieces.at[pl.ds(0, 2 * PLANE - 1)],
        0,
        {"dp": 1 - core, "wide": me},
    )
    others.wait_recv()
    others.wait_send()
    summed = pieces[0]
    for t in range(1, 2 * PLANE):
        summed = summed + pieces[t]
    zpieces[line] = summed
    for t in range(1, lines):
        meet(zpieces.at[line], zpieces.at[line], 1, {"wide": line_at[t] + spot}).start()
    others = meet(
        zpieces.at[pl.ds(0, lines - 1)],
        zpieces.at[pl.ds(0, lines - 1)],
        1,
        {"wide": line_at[1] + spot},
    )
    others.wait_recv()
    others.wait_send()
    summed = zpieces[0]
    for t in range(1, lines):
        summed = summed + zpieces[t]
    result[mine] = summed
    for t in range(PLANE):
        for c in (1, 0):
            if t or c:
                owner = lax.rem(core + c, 2)
                to = {"dp": owner, "wide": line_at[0] + spot_at(t)}
                meet(result.at[mine], result.at[mine], 2, to).start()

    for ch in range(CHUNKS):
        spread_rest(send2.at[ch], recv2.at[ch], CHUNKS + ch).wait_recv()
        arrived = recv2[ch].reshape(group, 4 * pad).T
        for i in range(2):
            got = dot_nt(
                arrived[2 * i * pad : 2 * (i + 1) * pad], legp[i, :, pl.ds(ch * group, group)]
            )
            if ch:
                got = got + out_acc[i]
            if ch < CHUNKS - 1:
                out_acc[i] = got
            else:
                spec_grad_ref[i] = jnp.concatenate(
                    [got[0:chans], got[pad : pad + chans]], axis=0
                ).astype(BF16)

    others = meet(
        result.at[pl.ds(0, 2 * PLANE - 1)],
        result.at[pl.ds(0, 2 * PLANE - 1)],
        2,
        {"dp": 1 - core, "wide": me},
    )
    others.wait_recv()
    others.wait_send()
    grad_in = result[pl.ds(0, PLANE)].reshape(pad, hid)
    gin_ref[...] = grad_in[0:chans]
    gbias_ref[...] = grad_in[chans : chans + 1]
    gout_ref[...] = result[pl.ds(PLANE, PLANE)].reshape(pad, hid)[0:chans]
    for ch in range(CHUNKS):
        spread_rest(send1.at[ch], recv1.at[ch], ch).wait_send()
        spread_rest(send2.at[ch], recv2.at[ch], CHUNKS + ch).wait_send()


def settle_kernel(*refs):
    count = (len(refs) - 2) // 3
    loads, stores = [], []
    for i in range(count):
        held = refs[2 * count + i]
        loads.append(pltpu.make_async_copy(refs[i], held, refs[-2].at[i]))
        stores.append(pltpu.make_async_copy(held, refs[count + i], refs[-1].at[i]))
        loads[i].start()
    for i in range(count):
        loads[i].wait()
        stores[i].start()
    for i in range(count):
        stores[i].wait()


def settle(*arrays):
    anywhere = pl.BlockSpec(memory_space=pl.ANY)
    sems = pltpu.SemaphoreType.DMA((len(arrays),))
    return pl.pallas_call(
        settle_kernel,
        name="settle",
        out_shape=[jax.ShapeDtypeStruct(x.shape, x.dtype) for x in arrays],
        in_specs=[anywhere] * len(arrays),
        out_specs=[anywhere] * len(arrays),
        scratch_shapes=[pltpu.VMEM(x.shape, x.dtype) for x in arrays] + [sems, sems],
        compiler_params=pltpu.CompilerParams(vmem_limit_bytes=56 * 2**20),
    )(*arrays)


def per_device(
    spec_cot, grid_state, weight_in, bias_in, weight_out, legendre, row_order, mode_order
):
    n = lax.axis_size("wide")
    _, rows, lon, chans = grid_state.shape
    hid = weight_in.shape[1]
    degrees = legendre.shape[1]
    pad = -(-(chans + 3) // 32) * 32
    total, group = rows * n, rows * n // CHUNKS
    per = rows // CHUNKS
    share = pad // PLANE // 2
    message = (CHUNKS, n, per, 4 * pad)
    scratch = [
        pltpu.VMEM((2, 2 * chans, degrees), BF16),
        pltpu.VMEM((chans, rows, lon), BF16),
        pltpu.VMEM((2, degrees, total), BF16),
        pltpu.VMEM((2, degrees, total), BF16),
        pltpu.VMEM((2 * pad, degrees), BF16),
        pltpu.VMEM((4 * pad, total), BF16),
        pltpu.VMEM((pad, hid), BF16),
        pltpu.VMEM((hid, pad), BF16),
        pltpu.VMEM((hid, pad), BF16),
        pltpu.VMEM((4 * n, lon), BF16),
        pltpu.VMEM((8, 4 * n), F32),
        pltpu.VMEM((rows, pad, lon), BF16),
        pltpu.VMEM((rows, hid, lon), F32),
        pltpu.VMEM((rows, hid, lon), BF16),
        pltpu.VMEM((per * pad, 4 * n), BF16),
        pltpu.VMEM((CHUNKS, per * pad, lon), BF16),
        pltpu.VMEM((per * pad, lon), BF16),
        pltpu.VMEM((4 * pad, group), BF16),
        pltpu.VMEM((2, 2 * pad, degrees), F32),
        pltpu.VMEM(message, BF16),
        pltpu.VMEM(message, BF16),
        pltpu.VMEM(message, BF16),
        pltpu.VMEM(message, BF16),
        pltpu.VMEM((2, pad, hid), F32),
        pltpu.VMEM((2, pad // 2, 2, hid), F32),
        pltpu.VMEM((2 * PLANE, share, 2, hid), F32),
        pltpu.VMEM((n // PLANE, share, 2, hid), F32),
        pltpu.VMEM((2 * PLANE, share, 2, hid), F32),
        pltpu.SemaphoreType.DMA((3,)),
        pltpu.SemaphoreType.DMA((2 * CHUNKS,)),
        pltpu.SemaphoreType.DMA((2 * CHUNKS,)),
        pltpu.SemaphoreType.DMA((3,)),
        pltpu.SemaphoreType.DMA((3,)),
        pltpu.SemaphoreType.REGULAR,
    ]
    vmem = pl.BlockSpec(memory_space=pltpu.VMEM)
    hbm = pl.BlockSpec(memory_space=pl.ANY)
    spec_grad, grad_in, grad_bias, grad_out = pl.pallas_call(
        functools.partial(step_kernel, (n, rows, chans, pad, lon, hid)),
        name="spectral_step",
        out_shape=(
            jax.ShapeDtypeStruct((2, 2 * chans, degrees), BF16),
            jax.ShapeDtypeStruct((chans, hid), F32),
            jax.ShapeDtypeStruct((1, hid), F32),
            jax.ShapeDtypeStruct((chans, hid), F32),
        ),
        in_specs=[hbm, hbm, vmem, vmem, vmem, hbm, vmem, vmem],
        out_specs=(vmem, vmem, vmem, vmem),
        scratch_shapes=scratch,
        compiler_params=pltpu.CompilerParams(
            collective_id=0, has_side_effects=True, vmem_limit_bytes=56 * 2**20
        ),
    )(
        jnp.swapaxes(spec_cot[0], 1, 2),
        jnp.transpose(grid_state[0], (2, 0, 1)),
        weight_in,
        bias_in.reshape(1, hid),
        weight_out.T,
        legendre,
        row_order.reshape(1, total),
        mode_order.reshape(1, 2 * n),
    )
    spec_grad, grad_in, grad_bias, grad_out = settle(spec_grad, grad_in, grad_bias, grad_out)
    return (
        jnp.swapaxes(spec_grad, 1, 2)[None],
        grad_in,
        grad_bias.reshape(hid),
        grad_out.T,
    )


def solution(mesh):
    placed = (
        P("dp", "wide", None, None),
        P("dp", "wide", None, None),
        P(),
        P(),
        P(),
        P("wide", None, None),
        P(),
        P(),
    )
    return jax.shard_map(
        per_device,
        mesh=mesh,
        in_specs=placed,
        out_specs=(P("dp", "wide", None, None), P(), P(), P()),
        check_vma=False,
    )
```

```python
import functools
import math

import jax
import jax.numpy as jnp
from jax import lax
from jax.experimental import pallas as pl
from jax.experimental.pallas import tpu as pltpu
from jax.sharding import PartitionSpec as P

MESH = pl.DeviceIdType.MESH
F32 = jnp.float32
BF16 = jnp.bfloat16
CHUNKS = 2
LANES = 128
PLANE = 16
TURN = 2.0 * math.pi


def dot(a, b):
    return jnp.dot(a, b, preferred_element_type=F32)


def dot_nt(a, b):
    return lax.dot_general(a, b, (((1,), (1,)), ((), ())), preferred_element_type=F32)


def iota(shape, axis):
    return lax.broadcasted_iota(jnp.int32, shape, axis)


def ones_where(mask):
    return jnp.where(mask, 1.0, 0.0).astype(BF16)


def step_kernel(
    sizes,
    spec_hbm,
    state_hbm,
    win_hbm,
    bias_hbm,
    wout_hbm,
    leg_hbm,
    rows_hbm,
    modes_hbm,
    spec_grad_ref,
    gin_ref,
    gbias_ref,
    gout_ref,
    spec_v,
    state_v,
    win_ref,
    bias_ref,
    wout_ref,
    leg_v,
    rows_ref,
    modes_ref,
    legp,
    spec_pad,
    coef,
    win_ext,
    win_t,
    wout_t,
    table,
    scale_v,
    columns,
    factor,
    active,
    lhs,
    grid_cot,
    grad_hidden,
    dstate,
    zbuf,
    out_acc,
    send1,
    recv1,
    send2,
    recv2,
    acc,
    part,
    pieces,
    zpieces,
    result,
    load_sem,
    a2a_send,
    a2a_recv,
    sum_send,
    sum_recv,
    ready,
):
    n, rows, chans, pad, lon, hid = sizes
    per = rows // CHUNKS
    group = per * n
    total = rows * n
    lines = n // PLANE
    me = lax.axis_index("wide")
    core = lax.axis_index("dp")
    line, spot = lax.div(me, PLANE), lax.rem(me, PLANE)
    line_at = [lax.rem(line + t, lines) * PLANE for t in range(lines)]

    def spot_at(t):
        return lax.rem(spot + t, PLANE)

    loads = [
        pltpu.make_async_copy(src, dst, load_sem.at[at])
        for at, (src, dst) in enumerate(
            [
                (leg_hbm, leg_v),
                (rows_hbm, rows_ref),
                (spec_hbm, spec_v),
                (modes_hbm, modes_ref),
                (state_hbm, state_v),
                (win_hbm, win_ref),
                (bias_hbm, bias_ref),
                (wout_hbm, wout_ref),
            ]
        )
    ]
    for load in loads:
        load.start()
    leg_load, rows_load, spec_load, modes_load, state_load, *weight_loads = loads

    barrier = pltpu.get_barrier_semaphore()
    for t in range(1, lines):
        pl.semaphore_signal(
            barrier, inc=1, device_id={"wide": line_at[t] + spot}, device_id_type=MESH
        )
    for t in range(1, PLANE):
        pl.semaphore_signal(
            barrier, inc=1, device_id={"wide": line_at[0] + spot_at(t)}, device_id_type=MESH
        )
    pl.semaphore_signal(
        barrier, inc=1, device_id={"dp": 1 - core, "wide": me}, device_id_type=MESH
    )

    def chunked(at):
        ch = lax.div(at, group)
        inner = at - ch * group
        owner = lax.div(inner, per)
        return owner * rows + ch * per + (inner - owner * per)

    order = ones_where(iota((total, total), 0) == chunked(iota((1, total), 1)))
    leg_load.wait()
    for i in range(2):
        legp[i] = dot(leg_v[i], order).astype(BF16)

    pl.semaphore_wait(barrier, lines + PLANE - 1)
    for t in range(1, PLANE):
        pl.semaphore_signal(
            ready, inc=1, device_id={"wide": line_at[0] + spot_at(t)}, device_id_type=MESH
        )

    rows_load.wait()
    row_at = rows_ref[...]
    north = jnp.minimum(row_at, total - 1 - row_at).astype(F32).astype(BF16)
    north = dot(jnp.broadcast_to(north, (16, total)), order)
    weights = jnp.sin((north[0:8] + 0.5) * (math.pi / total)) * (math.pi / total)
    spec_load.wait()
    zero_rows = jnp.zeros((pad - chans, spec_v.shape[2]), F32)
    for i in range(2):
        both = spec_v[i].astype(F32)
        spec_pad[i] = jnp.concatenate(
            [both[0:chans], zero_rows, both[chans : 2 * chans], zero_rows], axis=0
        ).astype(BF16)

    def to_messages(flat):
        return flat.reshape(n, per, 4 * pad)

    def spread(src, dst, slot, first=1, last=PLANE):
        def go(to):
            pltpu.make_async_remote_copy(
                src.at[to],
                dst.at[me],
                a2a_send.at[slot],
                a2a_recv.at[slot],
                device_id={"wide": to},
                device_id_type=MESH,
            ).start()

        if first == 1:
            for t in range(1, lines):
                go(line_at[t] + spot)

        @pl.loop(first, last)
        def _(t):
            at = spot_at(t)
            for s in range(lines):
                go(line_at[s] + at)

    def spread_rest(src, dst, slot):
        return pltpu.make_async_remote_copy(
            src.at[pl.ds(0, n - 1)],
            dst.at[pl.ds(0, n - 1)],
            a2a_send.at[slot],
            a2a_recv.at[slot],
            device_id={"wide": line_at[1] + spot},
            device_id_type=MESH,
        )

    for ch in range(CHUNKS):
        at = pl.ds(ch * group, group)
        for i in range(2):
            got = dot(spec_pad[i], legp[i, :, at])
            coef[pl.ds(i * 2 * pad, 2 * pad), :] = (
                got * weights[0:1, ch * group : (ch + 1) * group]
            ).astype(BF16)
        send1[ch] = to_messages(coef[...].T)
        recv1[ch, me] = send1[ch, me]
        if ch == 0:
            pl.semaphore_wait(ready, PLANE - 1)
        spread(send1.at[ch], recv1.at[ch], ch)

    for load in weight_loads:
        load.wait()
    win_rows = win_ref[...].astype(F32)
    bias = bias_ref[...]
    bias_parts = []
    for _ in range(3):
        high = bias.astype(BF16).astype(F32)
        bias_parts.append(high)
        bias = bias - high
    rest_rows = jnp.zeros((pad - chans - 3, hid), F32)
    extended = jnp.concatenate([win_rows] + bias_parts + [rest_rows], axis=0)
    win_ext[...] = extended.astype(BF16)
    win_t[...] = extended.T.astype(BF16)
    wout_rows = jnp.concatenate(
        [wout_ref[...].astype(F32), jnp.zeros((pad - chans, hid), F32)], axis=0
    )
    wout_t[...] = wout_rows.T.astype(BF16)

    state_load.wait()
    flat_state = state_v[...].reshape(chans * rows, lon)
    row_id = iota((pad, lon), 0)
    one_rows = jnp.logical_and(row_id >= chans, row_id < chans + 3)
    for j in range(rows):
        pick = ones_where(
            iota((pad, chans * rows), 1) == rows * iota((pad, chans * rows), 0) + j
        )
        columns[j] = jnp.where(one_rows, 1.0, dot(pick, flat_state)).astype(BF16)

    @pl.loop(0, rows)
    def _(j):
        preact = dot(win_t[...], columns[j])
        gate = jax.nn.sigmoid(preact)
        active[j] = (preact * gate).astype(BF16)
        factor[j] = gate * (1.0 + preact * (1.0 - gate))

    modes_load.wait()
    modes = modes_ref[...].astype(F32).astype(BF16)
    modes = jnp.broadcast_to(modes, (LANES, 2 * n))
    for i in range(2):
        choose = ones_where(iota((n, 2 * n), 1) == 2 * iota((n, 2 * n), 0) + i)
        mode = dot_nt(choose, modes)
        phase = mode * iota((n, LANES), 1).astype(F32)
        phase = phase - lon * jnp.floor(phase * (1.0 / lon))
        real, imag = jnp.cos(phase * (TURN / lon)), jnp.sin(phase * (TURN / lon))
        parts = lon // LANES
        jump = mode - parts * jnp.floor(mode * (1.0 / parts))
        jump_real, jump_imag = jnp.cos(jump * (TURN / parts)), jnp.sin(jump * (TURN / parts))
        for b in range(parts):
            at = pl.ds(b * LANES, LANES)
            table[pl.ds(2 * i * n, n), at] = real.astype(BF16)
            table[pl.ds((2 * i + 1) * n, n), at] = (-imag).astype(BF16)
            real, imag = real * jump_real - imag * jump_imag, imag * jump_real + real * jump_imag
    slot_modes = []
    for i in range(2):
        choose = ones_where(iota((2 * n, n), 0) == 2 * iota((2 * n, n), 1) + i)
        slot_modes += [dot(modes[0:16], choose)] * 2
    scale_v[...] = jnp.where(jnp.concatenate(slot_modes, axis=1) == 0.0, 1.0, 2.0)[0:8]

    def row_major(at):
        j = lax.div(at, n)
        return (at - j * n) * per + j

    regroup = ones_where(iota((group, group), 0) == row_major(iota((1, group), 1)))

    share = pad // PLANE // 2
    own_piece = core * PLANE + spot

    def meet(src, dst, slot, to):
        return pltpu.make_async_remote_copy(
            src,
            dst,
            sum_send.at[slot],
            sum_recv.at[slot],
            device_id=to,
            device_id_type=MESH,
        )

    def meet_rest(buffer, slot):
        count = buffer.shape[0] - 1
        rest = buffer.at[pl.ds(0, count)]
        return meet(rest, rest, slot, {"dp": 1 - core, "wide": me})

    def over_plane(source, target, slot, owners):
        for t in range(PLANE):
            for c in owners:
                at = spot_at(t)
                to = {"dp": c, "wide": line_at[0] + at}

                def go():
                    meet(source(c, at), target.at[own_piece], slot, to).start()

                if t:
                    go()
                else:
                    pl.when(core != c)(go)

    def sum_start(c):
        part[c] = acc[c].reshape(pad // 2, 2, hid)

        @pl.when(core == c)
        def _():
            pieces[own_piece] = part[c, pl.ds(spot * share, share)]

        over_plane(lambda c, s: part.at[c, pl.ds(s * share, share)], pieces, 0, (c,))

    def sum_middle():
        meet_rest(pieces, 0).wait_recv()
        summed = pieces[0]
        for t in range(1, 2 * PLANE):
            summed = summed + pieces[t]
        zpieces[line] = summed
        for t in range(1, lines):
            meet(zpieces.at[line], zpieces.at[line], 1, {"wide": line_at[t] + spot}).start()

    def sum_end():
        meet_rest(zpieces, 1).wait_recv()
        summed = zpieces[0]
        for t in range(1, lines):
            summed = summed + zpieces[t]
        result[own_piece] = summed.astype(BF16)
        over_plane(lambda c, s: result.at[own_piece], result, 2, (0, 1))

    for ch in range(CHUNKS):
        spread_rest(send1.at[ch], recv1.at[ch], ch).wait_recv()
        arrived = recv1[ch].reshape(group, 4 * pad).T
        arrived = dot(arrived, regroup).astype(BF16)
        for j in range(per):
            for q in range(4):
                lhs[pl.ds(j * pad, pad), pl.ds(q * n, n)] = arrived[
                    q * pad : (q + 1) * pad, j * n : (j + 1) * n
                ]
        grid_cot[ch] = (dot(lhs[...], table[...]) * (1.0 / lon)).astype(BF16)
        for j in range(per):
            row = ch * per + j
            grad = dot_nt(grid_cot[ch, pl.ds(j * pad, pad), :], active[row])
            acc[1] = grad if row == 0 else acc[1] + grad
        if ch == CHUNKS - 1:
            sum_start(1)
        for j in range(per):
            row = ch * per + j
            mine = pl.ds(j * pad, pad)
            grad_preact = (dot(wout_t[...], grid_cot[ch, mine, :]) * factor[row]).astype(BF16)
            grad_hidden[j] = grad_preact
            grad = dot_nt(columns[row], grad_preact)
            acc[0] = grad if row == 0 else acc[0] + grad
        if ch == CHUNKS - 1:
            sum_start(0)
        for j in range(per):
            dstate[pl.ds(j * pad, pad), :] = dot(win_ext[...], grad_hidden[j]).astype(BF16)
        back = (dot_nt(dstate[...], table[...]) * scale_v[0:1, :]).astype(BF16)
        for j in range(per):
            for q in range(4):
                zbuf[pl.ds(q * pad, pad), pl.ds(j * n, n)] = back[
                    j * pad : (j + 1) * pad, q * n : (q + 1) * n
                ]
        send2[ch] = to_messages(dot_nt(regroup, zbuf[...]).astype(BF16))
        recv2[ch, me] = send2[ch, me]
        if ch < CHUNKS - 1:
            spread(send2.at[ch], recv2.at[ch], CHUNKS + ch, 1, 16)
        else:
            spread(send2.at[ch], recv2.at[ch], CHUNKS + ch)
            sum_middle()
            sum_end()

    for ch in range(CHUNKS):
        spread_rest(send2.at[ch], recv2.at[ch], CHUNKS + ch).wait_recv()
        arrived = recv2[ch].reshape(group, 4 * pad).T
        for i in range(2):
            got = dot_nt(
                arrived[2 * i * pad : 2 * (i + 1) * pad], legp[i, :, pl.ds(ch * group, group)]
            )
            if ch:
                got = got + out_acc[i]
            if ch < CHUNKS - 1:
                out_acc[i] = got
            else:
                spec_grad_ref[i] = jnp.concatenate(
                    [got[0:chans], got[pad : pad + chans]], axis=0
                ).astype(BF16)

    meet_rest(result, 2).wait_recv()
    grad_in = result[pl.ds(0, PLANE)].astype(F32).reshape(pad, hid)
    gin_ref[...] = grad_in[0:chans]
    gbias_ref[...] = grad_in[chans : chans + 1]
    gout_ref[...] = result[pl.ds(PLANE, PLANE)].astype(F32).reshape(pad, hid)[0:chans]
    for ch in range(CHUNKS):
        spread_rest(send1.at[ch], recv1.at[ch], ch).wait_send()
        spread_rest(send2.at[ch], recv2.at[ch], CHUNKS + ch).wait_send()
    meet_rest(pieces, 0).wait_send()
    meet_rest(zpieces, 1).wait_send()
    meet_rest(result, 2).wait_send()


def settle_kernel(*refs):
    count = (len(refs) - 2) // 3
    loads, stores = [], []
    for i in range(count):
        held = refs[2 * count + i]
        loads.append(pltpu.make_async_copy(refs[i], held, refs[-2].at[i]))
        stores.append(pltpu.make_async_copy(held, refs[count + i], refs[-1].at[i]))
        loads[i].start()
    for i in range(count):
        loads[i].wait()
        stores[i].start()
    for i in range(count):
        stores[i].wait()


def settle(*arrays):
    anywhere = pl.BlockSpec(memory_space=pl.ANY)
    sems = pltpu.SemaphoreType.DMA((len(arrays),))
    return pl.pallas_call(
        settle_kernel,
        name="settle",
        out_shape=[jax.ShapeDtypeStruct(x.shape, x.dtype) for x in arrays],
        in_specs=[anywhere] * len(arrays),
        out_specs=[anywhere] * len(arrays),
        scratch_shapes=[pltpu.VMEM(x.shape, x.dtype) for x in arrays] + [sems, sems],
        compiler_params=pltpu.CompilerParams(vmem_limit_bytes=56 * 2**20),
    )(*arrays)


def per_device(
    spec_cot, grid_state, weight_in, bias_in, weight_out, legendre, row_order, mode_order
):
    n = lax.axis_size("wide")
    _, rows, lon, chans = grid_state.shape
    hid = weight_in.shape[1]
    degrees = legendre.shape[1]
    pad = -(-(chans + 3) // 32) * 32
    total, group = rows * n, rows * n // CHUNKS
    per = rows // CHUNKS
    share = pad // PLANE // 2
    message = (CHUNKS, n, per, 4 * pad)
    scratch = [
        pltpu.VMEM((2, 2 * chans, degrees), BF16),
        pltpu.VMEM((chans, rows, lon), BF16),
        pltpu.VMEM((chans, hid), BF16),
        pltpu.VMEM((1, hid), F32),
        pltpu.VMEM((chans, hid), BF16),
        pltpu.VMEM((2, degrees, total), BF16),
        pltpu.VMEM((1, total), jnp.int32),
        pltpu.VMEM((1, 2 * n), jnp.int32),
        pltpu.VMEM((2, degrees, total), BF16),
        pltpu.VMEM((2, 2 * pad, degrees), BF16),
        pltpu.VMEM((4 * pad, group), BF16),
        pltpu.VMEM((pad, hid), BF16),
        pltpu.VMEM((hid, pad), BF16),
        pltpu.VMEM((hid, pad), BF16),
        pltpu.VMEM((4 * n, lon), BF16),
        pltpu.VMEM((8, 4 * n), F32),
        pltpu.VMEM((rows, pad, lon), BF16),
        pltpu.VMEM((rows, hid, lon), F32),
        pltpu.VMEM((rows, hid, lon), BF16),
        pltpu.VMEM((per * pad, 4 * n), BF16),
        pltpu.VMEM((CHUNKS, per * pad, lon), BF16),
        pltpu.VMEM((per, hid, lon), BF16),
        pltpu.VMEM((per * pad, lon), BF16),
        pltpu.VMEM((4 * pad, group), BF16),
        pltpu.VMEM((2, 2 * pad, degrees), F32),
        pltpu.VMEM(message, BF16),
        pltpu.VMEM(message, BF16),
        pltpu.VMEM(message, BF16),
        pltpu.VMEM(message, BF16),
        pltpu.VMEM((2, pad, hid), F32),
        pltpu.VMEM((2, pad // 2, 2, hid), F32),
        pltpu.VMEM((2 * PLANE, share, 2, hid), F32),
        pltpu.VMEM((n // PLANE, share, 2, hid), F32),
        pltpu.VMEM((2 * PLANE, share, 2, hid), BF16),
        pltpu.SemaphoreType.DMA((8,)),
        pltpu.SemaphoreType.DMA((2 * CHUNKS,)),
        pltpu.SemaphoreType.DMA((2 * CHUNKS,)),
        pltpu.SemaphoreType.DMA((3,)),
        pltpu.SemaphoreType.DMA((3,)),
        pltpu.SemaphoreType.REGULAR,
    ]
    vmem = pl.BlockSpec(memory_space=pltpu.VMEM)
    hbm = pl.BlockSpec(memory_space=pl.ANY)
    spec_grad, grad_in, grad_bias, grad_out = pl.pallas_call(
        functools.partial(step_kernel, (n, rows, chans, pad, lon, hid)),
        name="spectral_step",
        out_shape=(
            jax.ShapeDtypeStruct((2, 2 * chans, degrees), BF16),
            jax.ShapeDtypeStruct((chans, hid), F32),
            jax.ShapeDtypeStruct((1, hid), F32),
            jax.ShapeDtypeStruct((chans, hid), F32),
        ),
        in_specs=[hbm] * 8,
        out_specs=(vmem, vmem, vmem, vmem),
        scratch_shapes=scratch,
        compiler_params=pltpu.CompilerParams(
            collective_id=0, has_side_effects=True, vmem_limit_bytes=56 * 2**20
        ),
    )(
        jnp.swapaxes(spec_cot[0], 1, 2),
        jnp.transpose(grid_state[0], (2, 0, 1)),
        weight_in,
        bias_in.reshape(1, hid),
        weight_out.T,
        legendre,
        row_order.reshape(1, total),
        mode_order.reshape(1, 2 * n),
    )
    spec_grad, grad_in, grad_bias, grad_out = settle(spec_grad, grad_in, grad_bias, grad_out)
    return (
        jnp.swapaxes(spec_grad, 1, 2)[None],
        grad_in,
        grad_bias.reshape(hid),
        grad_out.T,
    )


def solution(mesh):
    placed = (
        P("dp", "wide", None, None),
        P("dp", "wide", None, None),
        P(),
        P(),
        P(),
        P("wide", None, None),
        P(),
        P(),
    )
    return jax.shard_map(
        per_device,
        mesh=mesh,
        in_specs=placed,
        out_specs=(P("dp", "wide", None, None), P(), P(), P()),
        check_vma=False,
    )
```

```python
import functools
import math

import jax
import jax.numpy as jnp
from jax import lax
from jax.experimental import pallas as pl
from jax.experimental.pallas import tpu as pltpu
from jax.sharding import PartitionSpec as P

MESH = pl.DeviceIdType.MESH
F32 = jnp.float32
BF16 = jnp.bfloat16
CHUNKS = 2
LANES = 128
PLANE = 16
TURN = 2.0 * math.pi


def dot(a, b):
    return jnp.dot(a, b, preferred_element_type=F32)


def dot_nt(a, b):
    return lax.dot_general(a, b, (((1,), (1,)), ((), ())), preferred_element_type=F32)


def iota(shape, axis):
    return lax.broadcasted_iota(jnp.int32, shape, axis)


def ones_where(mask):
    return jnp.where(mask, 1.0, 0.0).astype(BF16)


def step_kernel(
    sizes,
    spec_hbm,
    state_hbm,
    win_hbm,
    bias_hbm,
    wout_hbm,
    leg_hbm,
    rows_hbm,
    modes_hbm,
    spec_grad_ref,
    sums_ref,
    spec_out_v,
    spec_v,
    state_v,
    win_ref,
    bias_ref,
    wout_ref,
    leg_v,
    rows_ref,
    modes_ref,
    legp,
    spec_pad,
    coef,
    win_ext,
    win_t,
    wout_t,
    table,
    scale_v,
    columns,
    factor,
    active,
    lhs,
    grid_cot,
    grad_hidden,
    dstate,
    zbuf,
    out_acc,
    send1,
    recv1,
    send2,
    recv2,
    acc,
    part,
    pieces,
    zpieces,
    result,
    load_sem,
    a2a_send,
    a2a_recv,
    sum_send,
    sum_recv,
    ready,
):
    n, rows, chans, pad, lon, hid = sizes
    per = rows // CHUNKS
    group = per * n
    total = rows * n
    lines = n // PLANE
    me = lax.axis_index("wide")
    core = lax.axis_index("dp")
    line, spot = lax.div(me, PLANE), lax.rem(me, PLANE)
    line_at = [lax.rem(line + t, lines) * PLANE for t in range(lines)]

    def spot_at(t):
        return lax.rem(spot + t, PLANE)

    loads = [
        pltpu.make_async_copy(src, dst, load_sem.at[at])
        for at, (src, dst) in enumerate(
            [
                (leg_hbm, leg_v),
                (rows_hbm, rows_ref),
                (spec_hbm, spec_v),
                (modes_hbm, modes_ref),
                (state_hbm, state_v),
                (win_hbm, win_ref),
                (bias_hbm, bias_ref),
                (wout_hbm, wout_ref),
            ]
        )
    ]
    for load in loads:
        load.start()
    leg_load, rows_load, spec_load, modes_load, state_load, *weight_loads = loads

    barrier = pltpu.get_barrier_semaphore()
    for t in range(1, lines):
        pl.semaphore_signal(
            barrier, inc=1, device_id={"wide": line_at[t] + spot}, device_id_type=MESH
        )
    for t in range(1, PLANE):
        pl.semaphore_signal(
            barrier, inc=1, device_id={"wide": line_at[0] + spot_at(t)}, device_id_type=MESH
        )
    pl.semaphore_signal(
        barrier, inc=1, device_id={"dp": 1 - core, "wide": me}, device_id_type=MESH
    )

    def chunked(at):
        ch = lax.div(at, group)
        inner = at - ch * group
        owner = lax.div(inner, per)
        return owner * rows + ch * per + (inner - owner * per)

    order = ones_where(iota((total, total), 0) == chunked(iota((1, total), 1)))
    leg_load.wait()
    for i in range(2):
        legp[i] = dot(leg_v[i], order).astype(BF16)

    pl.semaphore_wait(barrier, lines + PLANE - 1)
    for t in range(1, PLANE):
        pl.semaphore_signal(
            ready, inc=1, device_id={"wide": line_at[0] + spot_at(t)}, device_id_type=MESH
        )

    rows_load.wait()
    row_at = rows_ref[...]
    north = jnp.minimum(row_at, total - 1 - row_at).astype(F32).astype(BF16)
    north = dot(jnp.broadcast_to(north, (16, total)), order)
    weights = jnp.sin((north[0:8] + 0.5) * (math.pi / total)) * (math.pi / total)
    spec_load.wait()
    zero_rows = jnp.zeros((pad - chans, spec_v.shape[2]), F32)
    for i in range(2):
        both = spec_v[i].astype(F32)
        spec_pad[i] = jnp.concatenate(
            [both[0:chans], zero_rows, both[chans : 2 * chans], zero_rows], axis=0
        ).astype(BF16)

    def to_messages(flat):
        return flat.reshape(n, per, 4 * pad)

    def spread(src, dst, slot, first=1, last=PLANE):
        def go(to):
            pltpu.make_async_remote_copy(
                src.at[to],
                dst.at[me],
                a2a_send.at[slot],
                a2a_recv.at[slot],
                device_id={"wide": to},
                device_id_type=MESH,
            ).start()

        if first == 1:
            for t in range(1, lines):
                go(line_at[t] + spot)

        @pl.loop(first, last)
        def _(t):
            at = spot_at(t)
            for s in range(lines):
                go(line_at[s] + at)

    def spread_rest(src, dst, slot):
        return pltpu.make_async_remote_copy(
            src.at[pl.ds(0, n - 1)],
            dst.at[pl.ds(0, n - 1)],
            a2a_send.at[slot],
            a2a_recv.at[slot],
            device_id={"wide": line_at[1] + spot},
            device_id_type=MESH,
        )

    for ch in range(CHUNKS):
        at = pl.ds(ch * group, group)
        for i in range(2):
            got = dot(spec_pad[i], legp[i, :, at])
            coef[pl.ds(i * 2 * pad, 2 * pad), :] = (
                got * weights[0:1, ch * group : (ch + 1) * group]
            ).astype(BF16)
        send1[ch] = to_messages(coef[...].T)
        recv1[ch, me] = send1[ch, me]
        if ch == 0:
            pl.semaphore_wait(ready, PLANE - 1)
        spread(send1.at[ch], recv1.at[ch], ch)

    for load in weight_loads:
        load.wait()
    win_rows = win_ref[...].astype(F32)
    bias = bias_ref[...]
    bias_parts = []
    for _ in range(3):
        high = bias.astype(BF16).astype(F32)
        bias_parts.append(high)
        bias = bias - high
    rest_rows = jnp.zeros((pad - chans - 3, hid), F32)
    extended = jnp.concatenate([win_rows] + bias_parts + [rest_rows], axis=0)
    win_ext[...] = extended.astype(BF16)
    win_t[...] = extended.T.astype(BF16)
    wout_rows = jnp.concatenate(
        [wout_ref[...].astype(F32), jnp.zeros((pad - chans, hid), F32)], axis=0
    )
    wout_t[...] = wout_rows.T.astype(BF16)

    state_load.wait()
    flat_state = state_v[...].reshape(chans * rows, lon)
    row_id = iota((pad, lon), 0)
    one_rows = jnp.logical_and(row_id >= chans, row_id < chans + 3)
    for j in range(rows):
        pick = ones_where(
            iota((pad, chans * rows), 1) == rows * iota((pad, chans * rows), 0) + j
        )
        columns[j] = jnp.where(one_rows, 1.0, dot(pick, flat_state)).astype(BF16)

    @pl.loop(0, rows)
    def _(j):
        preact = dot(win_t[...], columns[j])
        gate = jax.nn.sigmoid(preact)
        active[j] = (preact * gate).astype(BF16)
        factor[j] = gate * (1.0 + preact * (1.0 - gate))

    modes_load.wait()
    modes = modes_ref[...].astype(F32).astype(BF16)
    modes = jnp.broadcast_to(modes, (LANES, 2 * n))
    for i in range(2):
        choose = ones_where(iota((n, 2 * n), 1) == 2 * iota((n, 2 * n), 0) + i)
        mode = dot_nt(choose, modes)
        phase = mode * iota((n, LANES), 1).astype(F32)
        phase = phase - lon * jnp.floor(phase * (1.0 / lon))
        real, imag = jnp.cos(phase * (TURN / lon)), jnp.sin(phase * (TURN / lon))
        parts = lon // LANES
        jump = mode - parts * jnp.floor(mode * (1.0 / parts))
        jump_real, jump_imag = jnp.cos(jump * (TURN / parts)), jnp.sin(jump * (TURN / parts))
        for b in range(parts):
            at = pl.ds(b * LANES, LANES)
            table[pl.ds(2 * i * n, n), at] = real.astype(BF16)
            table[pl.ds((2 * i + 1) * n, n), at] = (-imag).astype(BF16)
            real, imag = real * jump_real - imag * jump_imag, imag * jump_real + real * jump_imag
    slot_modes = []
    for i in range(2):
        choose = ones_where(iota((2 * n, n), 0) == 2 * iota((2 * n, n), 1) + i)
        slot_modes += [dot(modes[0:16], choose)] * 2
    scale_v[...] = jnp.where(jnp.concatenate(slot_modes, axis=1) == 0.0, 1.0, 2.0)[0:8]

    def row_major(at):
        j = lax.div(at, n)
        return (at - j * n) * per + j

    regroup = ones_where(iota((group, group), 0) == row_major(iota((1, group), 1)))

    share = pad // PLANE // 2
    own_piece = core * PLANE + spot

    def meet(src, dst, slot, to):
        return pltpu.make_async_remote_copy(
            src,
            dst,
            sum_send.at[slot],
            sum_recv.at[slot],
            device_id=to,
            device_id_type=MESH,
        )

    def meet_rest(buffer, slot):
        count = buffer.shape[0] - 1
        rest = buffer.at[pl.ds(0, count)]
        return meet(rest, rest, slot, {"dp": 1 - core, "wide": me})

    def over_plane(source, target, slot, owners):
        for t in range(PLANE):
            for c in owners:
                at = spot_at(t)
                to = {"dp": c, "wide": line_at[0] + at}

                def go():
                    meet(source(c, at), target.at[own_piece], slot, to).start()

                if t:
                    go()
                else:
                    pl.when(core != c)(go)

    def sum_start(c):
        part[c] = acc[c].reshape(pad // 2, 2, hid)

        @pl.when(core == c)
        def _():
            pieces[own_piece] = part[c, pl.ds(spot * share, share)]

        over_plane(lambda c, s: part.at[c, pl.ds(s * share, share)], pieces, 0, (c,))

    def sum_middle():
        meet_rest(pieces, 0).wait_recv()
        summed = pieces[0]
        for t in range(1, 2 * PLANE):
            summed = summed + pieces[t]
        zpieces[line] = summed
        for t in range(1, lines):
            meet(zpieces.at[line], zpieces.at[line], 1, {"wide": line_at[t] + spot}).start()

    def sum_end():
        meet_rest(zpieces, 1).wait_recv()
        summed = zpieces[0]
        for t in range(1, lines):
            summed = summed + zpieces[t]
        result[own_piece] = summed.astype(BF16)
        over_plane(lambda c, s: result.at[own_piece], result, 2, (0, 1))

    def gather_out(ch):
        for j in range(per):
            row = ch * per + j
            grad = dot_nt(grid_cot[ch, pl.ds(j * pad, pad), :], active[row])
            acc[1] = grad if row == 0 else acc[1] + grad

    def gather_in(ch):
        for j in range(per):
            row = ch * per + j
            grad = dot_nt(columns[row], grad_hidden[j])
            acc[0] = grad if row == 0 else acc[0] + grad

    for ch in range(CHUNKS):
        spread_rest(send1.at[ch], recv1.at[ch], ch).wait_recv()
        arrived = recv1[ch].reshape(group, 4 * pad).T
        arrived = dot(arrived, regroup).astype(BF16)
        for j in range(per):
            for q in range(4):
                lhs[pl.ds(j * pad, pad), pl.ds(q * n, n)] = arrived[
                    q * pad : (q + 1) * pad, j * n : (j + 1) * n
                ]
        grid_cot[ch] = (dot(lhs[...], table[...]) * (1.0 / lon)).astype(BF16)
        last = ch == CHUNKS - 1
        if last:
            gather_out(ch)
            sum_start(1)
        for j in range(per):
            cot_row = grid_cot[ch, pl.ds(j * pad, pad), :]
            back_hidden = dot(wout_t[...], cot_row)
            grad_hidden[j] = (back_hidden * factor[ch * per + j]).astype(BF16)
        if last:
            gather_in(ch)
            sum_start(0)
        for j in range(per):
            dstate[pl.ds(j * pad, pad), :] = dot(win_ext[...], grad_hidden[j]).astype(BF16)
        back = (dot_nt(dstate[...], table[...]) * scale_v[0:1, :]).astype(BF16)
        for j in range(per):
            for q in range(4):
                zbuf[pl.ds(q * pad, pad), pl.ds(j * n, n)] = back[
                    j * pad : (j + 1) * pad, q * n : (q + 1) * n
                ]
        send2[ch] = to_messages(dot_nt(regroup, zbuf[...]).astype(BF16))
        recv2[ch, me] = send2[ch, me]
        spread(send2.at[ch], recv2.at[ch], CHUNKS + ch)
        if last:
            sum_middle()
            sum_end()
        else:
            gather_out(ch)
            gather_in(ch)

    for ch in range(CHUNKS):
        spread_rest(send2.at[ch], recv2.at[ch], CHUNKS + ch).wait_recv()
        arrived = recv2[ch].reshape(group, 4 * pad).T
        for i in range(2):
            got = dot_nt(
                arrived[2 * i * pad : 2 * (i + 1) * pad], legp[i, :, pl.ds(ch * group, group)]
            )
            if ch:
                got = got + out_acc[i]
            if ch < CHUNKS - 1:
                out_acc[i] = got
            else:
                spec_out_v[i] = jnp.concatenate(
                    [got[0:chans], got[pad : pad + chans]], axis=0
                ).astype(BF16)

    spec_out = pltpu.make_async_copy(spec_out_v, spec_grad_ref, load_sem.at[0])
    spec_out.start()
    meet_rest(result, 2).wait_recv()
    sums_out = pltpu.make_async_copy(result, sums_ref, load_sem.at[1])
    sums_out.start()
    for ch in range(CHUNKS):
        spread_rest(send1.at[ch], recv1.at[ch], ch).wait_send()
        spread_rest(send2.at[ch], recv2.at[ch], CHUNKS + ch).wait_send()
    meet_rest(pieces, 0).wait_send()
    meet_rest(zpieces, 1).wait_send()
    meet_rest(result, 2).wait_send()
    sums_out.wait()
    spec_out.wait()


def settle_kernel(
    spec_hbm,
    sums_hbm,
    spec_out,
    gin_out,
    gbias_out,
    gout_out,
    spec_v,
    sums_v,
    gin_v,
    gbias_v,
    gout_v,
    load_sem,
    store_sem,
):
    chans, hid = gin_v.shape
    spec_load = pltpu.make_async_copy(spec_hbm, spec_v, load_sem.at[0])
    sums_load = pltpu.make_async_copy(sums_hbm, sums_v, load_sem.at[1])
    stores = [
        pltpu.make_async_copy(src, dst, store_sem.at[at])
        for at, (src, dst) in enumerate(
            [(spec_v, spec_out), (gin_v, gin_out), (gbias_v, gbias_out), (gout_v, gout_out)]
        )
    ]
    sums_load.start()
    spec_load.start()
    half = sums_v.shape[0] // 2
    pad = half * sums_v.shape[1] * 2
    sums_load.wait()
    grad_in = sums_v[pl.ds(0, half)].astype(F32).reshape(pad, hid)
    gin_v[...] = grad_in[0:chans]
    gbias_v[...] = grad_in[chans : chans + 1]
    stores[1].start()
    stores[2].start()
    gout_v[...] = sums_v[pl.ds(half, half)].astype(F32).reshape(pad, hid)[0:chans]
    stores[3].start()
    spec_load.wait()
    stores[0].start()
    for store in stores:
        store.wait()


def settle(spec_grad, sums, chans, hid):
    anywhere = pl.BlockSpec(memory_space=pl.ANY)
    shapes = [
        jax.ShapeDtypeStruct(spec_grad.shape, spec_grad.dtype),
        jax.ShapeDtypeStruct((chans, hid), F32),
        jax.ShapeDtypeStruct((1, hid), F32),
        jax.ShapeDtypeStruct((chans, hid), F32),
    ]
    held = [spec_grad, sums] + shapes[1:]
    return pl.pallas_call(
        settle_kernel,
        name="settle",
        out_shape=shapes,
        in_specs=[anywhere] * 2,
        out_specs=[anywhere] * 4,
        scratch_shapes=[pltpu.VMEM(x.shape, x.dtype) for x in held]
        + [pltpu.SemaphoreType.DMA((2,)), pltpu.SemaphoreType.DMA((4,))],
        compiler_params=pltpu.CompilerParams(vmem_limit_bytes=56 * 2**20),
    )(spec_grad, sums)


def per_device(
    spec_cot, grid_state, weight_in, bias_in, weight_out, legendre, row_order, mode_order
):
    n = lax.axis_size("wide")
    _, rows, lon, chans = grid_state.shape
    hid = weight_in.shape[1]
    degrees = legendre.shape[1]
    pad = -(-(chans + 3) // 32) * 32
    total, group = rows * n, rows * n // CHUNKS
    per = rows // CHUNKS
    share = pad // PLANE // 2
    message = (CHUNKS, n, per, 4 * pad)
    scratch = [
        pltpu.VMEM((2, 2 * chans, degrees), BF16),
        pltpu.VMEM((2, 2 * chans, degrees), BF16),
        pltpu.VMEM((chans, rows, lon), BF16),
        pltpu.VMEM((chans, hid), BF16),
        pltpu.VMEM((1, hid), F32),
        pltpu.VMEM((chans, hid), BF16),
        pltpu.VMEM((2, degrees, total), BF16),
        pltpu.VMEM((1, total), jnp.int32),
        pltpu.VMEM((1, 2 * n), jnp.int32),
        pltpu.VMEM((2, degrees, total), BF16),
        pltpu.VMEM((2, 2 * pad, degrees), BF16),
        pltpu.VMEM((4 * pad, group), BF16),
        pltpu.VMEM((pad, hid), BF16),
        pltpu.VMEM((hid, pad), BF16),
        pltpu.VMEM((hid, pad), BF16),
        pltpu.VMEM((4 * n, lon), BF16),
        pltpu.VMEM((8, 4 * n), F32),
        pltpu.VMEM((rows, pad, lon), BF16),
        pltpu.VMEM((rows, hid, lon), F32),
        pltpu.VMEM((rows, hid, lon), BF16),
        pltpu.VMEM((per * pad, 4 * n), BF16),
        pltpu.VMEM((CHUNKS, per * pad, lon), BF16),
        pltpu.VMEM((per, hid, lon), BF16),
        pltpu.VMEM((per * pad, lon), BF16),
        pltpu.VMEM((4 * pad, group), BF16),
        pltpu.VMEM((2, 2 * pad, degrees), F32),
        pltpu.VMEM(message, BF16),
        pltpu.VMEM(message, BF16),
        pltpu.VMEM(message, BF16),
        pltpu.VMEM(message, BF16),
        pltpu.VMEM((2, pad, hid), F32),
        pltpu.VMEM((2, pad // 2, 2, hid), F32),
        pltpu.VMEM((2 * PLANE, share, 2, hid), F32),
        pltpu.VMEM((n // PLANE, share, 2, hid), F32),
        pltpu.VMEM((2 * PLANE, share, 2, hid), BF16),
        pltpu.SemaphoreType.DMA((8,)),
        pltpu.SemaphoreType.DMA((2 * CHUNKS,)),
        pltpu.SemaphoreType.DMA((2 * CHUNKS,)),
        pltpu.SemaphoreType.DMA((3,)),
        pltpu.SemaphoreType.DMA((3,)),
        pltpu.SemaphoreType.REGULAR,
    ]
    hbm = pl.BlockSpec(memory_space=pl.ANY)
    spec_grad, sums = pl.pallas_call(
        functools.partial(step_kernel, (n, rows, chans, pad, lon, hid)),
        name="spectral_step",
        out_shape=(
            jax.ShapeDtypeStruct((2, 2 * chans, degrees), BF16),
            jax.ShapeDtypeStruct((2 * PLANE, share, 2, hid), BF16),
        ),
        in_specs=[hbm] * 8,
        out_specs=(hbm, hbm),
        scratch_shapes=scratch,
        compiler_params=pltpu.CompilerParams(
            collective_id=0, has_side_effects=True, vmem_limit_bytes=56 * 2**20
        ),
    )(
        jnp.swapaxes(spec_cot[0], 1, 2),
        jnp.transpose(grid_state[0], (2, 0, 1)),
        weight_in,
        bias_in.reshape(1, hid),
        weight_out.T,
        legendre,
        row_order.reshape(1, total),
        mode_order.reshape(1, 2 * n),
    )
    spec_grad, grad_in, grad_bias, grad_out = settle(spec_grad, sums, chans, hid)
    return (
        jnp.swapaxes(spec_grad, 1, 2)[None],
        grad_in,
        grad_bias.reshape(hid),
        grad_out.T,
    )


def solution(mesh):
    placed = (
        P("dp", "wide", None, None),
        P("dp", "wide", None, None),
        P(),
        P(),
        P(),
        P("wide", None, None),
        P(),
        P(),
    )
    return jax.shard_map(
        per_device,
        mesh=mesh,
        in_specs=placed,
        out_specs=(P("dp", "wide", None, None), P(), P(), P()),
        check_vma=False,
    )
```

```python
import functools
import math

import jax
import jax.numpy as jnp
from jax import lax
from jax.experimental import pallas as pl
from jax.experimental.pallas import tpu as pltpu
from jax.sharding import PartitionSpec as P

MESH = pl.DeviceIdType.MESH
F32 = jnp.float32
BF16 = jnp.bfloat16
CHUNKS = 2
LANES = 128
PLANE = 16
TURN = 2.0 * math.pi


def dot(a, b):
    return jnp.dot(a, b, preferred_element_type=F32)


def dot_nt(a, b):
    return lax.dot_general(a, b, (((1,), (1,)), ((), ())), preferred_element_type=F32)


def iota(shape, axis):
    return lax.broadcasted_iota(jnp.int32, shape, axis)


def ones_where(mask):
    return jnp.where(mask, 1.0, 0.0).astype(BF16)


def step_kernel(
    sizes,
    spec_hbm,
    state_hbm,
    win_hbm,
    bias_hbm,
    wout_hbm,
    leg_hbm,
    rows_hbm,
    modes_hbm,
    spec_grad_ref,
    sums_ref,
    spec_out_v,
    spec_v,
    state_v,
    win_ref,
    bias_ref,
    wout_ref,
    leg_v,
    rows_ref,
    modes_ref,
    legp,
    spec_pad,
    coef,
    win_ext,
    win_t,
    wout_t,
    table,
    scale_v,
    columns,
    factor,
    active,
    lhs,
    grid_cot,
    grad_hidden,
    dstate,
    zbuf,
    out_acc,
    send1,
    recv1,
    send2,
    recv2,
    acc,
    part,
    pieces,
    zpieces,
    result,
    load_sem,
    a2a_send,
    a2a_recv,
    sum_send,
    sum_recv,
    ready,
):
    n, rows, chans, pad, lon, hid = sizes
    per = rows // CHUNKS
    group = per * n
    total = rows * n
    lines = n // PLANE
    me = lax.axis_index("wide")
    core = lax.axis_index("dp")
    line, spot = lax.div(me, PLANE), lax.rem(me, PLANE)
    line_at = [lax.rem(line + t, lines) * PLANE for t in range(lines)]

    def spot_at(t):
        return lax.rem(spot + t, PLANE)

    loads = [
        pltpu.make_async_copy(src, dst, load_sem.at[at])
        for at, (src, dst) in enumerate(
            [
                (leg_hbm, leg_v),
                (rows_hbm, rows_ref),
                (spec_hbm, spec_v),
                (modes_hbm, modes_ref),
                (state_hbm, state_v),
                (win_hbm, win_ref),
                (bias_hbm, bias_ref),
                (wout_hbm, wout_ref),
            ]
        )
    ]
    for load in loads:
        load.start()
    leg_load, rows_load, spec_load, modes_load, state_load, *weight_loads = loads

    barrier = pltpu.get_barrier_semaphore()
    for t in range(1, lines):
        pl.semaphore_signal(
            barrier, inc=1, device_id={"wide": line_at[t] + spot}, device_id_type=MESH
        )
    for t in range(1, PLANE):
        pl.semaphore_signal(
            barrier, inc=1, device_id={"wide": line_at[0] + spot_at(t)}, device_id_type=MESH
        )
    pl.semaphore_signal(
        barrier, inc=1, device_id={"dp": 1 - core, "wide": me}, device_id_type=MESH
    )

    pl.semaphore_wait(barrier, lines + PLANE - 1)
    for t in range(1, PLANE):
        pl.semaphore_signal(
            ready, inc=1, device_id={"wide": line_at[0] + spot_at(t)}, device_id_type=MESH
        )

    rows_load.wait()
    row_at = rows_ref[...]
    north = jnp.minimum(row_at, total - 1 - row_at).astype(F32)
    weights = jnp.sin((north + 0.5) * (math.pi / total)) * (math.pi / total)
    spec_load.wait()
    zero_rows = jnp.zeros((pad - chans, spec_v.shape[2]), F32)
    for i in range(2):
        both = spec_v[i].astype(F32)
        spec_pad[i] = jnp.concatenate(
            [both[0:chans], zero_rows, both[chans : 2 * chans], zero_rows], axis=0
        ).astype(BF16)

    def to_messages(flat):
        return flat.reshape(n, flat.shape[0] // n, 4 * pad)

    def spread(src, dst, slot, first=1, last=PLANE):
        def go(to):
            pltpu.make_async_remote_copy(
                src.at[to],
                dst.at[me],
                a2a_send.at[slot],
                a2a_recv.at[slot],
                device_id={"wide": to},
                device_id_type=MESH,
            ).start()

        if first == 1:
            for t in range(1, lines):
                go(line_at[t] + spot)

        @pl.loop(first, last)
        def _(t):
            at = spot_at(t)
            for s in range(lines):
                go(line_at[s] + at)

    def spread_rest(src, dst, slot):
        return pltpu.make_async_remote_copy(
            src.at[pl.ds(0, n - 1)],
            dst.at[pl.ds(0, n - 1)],
            a2a_send.at[slot],
            a2a_recv.at[slot],
            device_id={"wide": line_at[1] + spot},
            device_id_type=MESH,
        )

    leg_load.wait()
    for i in range(2):
        got = dot(spec_pad[i], leg_v[i])
        coef[pl.ds(i * 2 * pad, 2 * pad), :] = (got * weights).astype(BF16)
    messages = to_messages(coef[...].T)
    for ch in range(CHUNKS):
        send1[ch] = messages[:, ch * per : (ch + 1) * per]
        recv1[ch, me] = send1[ch, me]
    pl.semaphore_wait(ready, PLANE - 1)
    for ch in range(CHUNKS):
        spread(send1.at[ch], recv1.at[ch], ch)

    def chunked(at):
        ch = lax.div(at, group)
        inner = at - ch * group
        owner = lax.div(inner, per)
        return owner * rows + ch * per + (inner - owner * per)

    order = ones_where(iota((total, total), 0) == chunked(iota((1, total), 1)))
    for i in range(2):
        legp[i] = dot(leg_v[i], order).astype(BF16)

    for load in weight_loads:
        load.wait()
    win_rows = win_ref[...].astype(F32)
    bias = bias_ref[...]
    bias_parts = []
    for _ in range(3):
        high = bias.astype(BF16).astype(F32)
        bias_parts.append(high)
        bias = bias - high
    rest_rows = jnp.zeros((pad - chans - 3, hid), F32)
    extended = jnp.concatenate([win_rows] + bias_parts + [rest_rows], axis=0)
    win_ext[...] = extended.astype(BF16)
    win_t[...] = extended.T.astype(BF16)
    wout_rows = jnp.concatenate(
        [wout_ref[...].astype(F32), jnp.zeros((pad - chans, hid), F32)], axis=0
    )
    wout_t[...] = wout_rows.T.astype(BF16)

    state_load.wait()
    flat_state = state_v[...].reshape(chans * rows, lon)
    row_id = iota((pad, lon), 0)
    one_rows = jnp.logical_and(row_id >= chans, row_id < chans + 3)
    for j in range(rows):
        pick = ones_where(
            iota((pad, chans * rows), 1) == rows * iota((pad, chans * rows), 0) + j
        )
        columns[j] = jnp.where(one_rows, 1.0, dot(pick, flat_state)).astype(BF16)

    @pl.loop(0, rows)
    def _(j):
        preact = dot(win_t[...], columns[j])
        gate = jax.nn.sigmoid(preact)
        active[j] = (preact * gate).astype(BF16)
        factor[j] = gate * (1.0 + preact * (1.0 - gate))

    modes_load.wait()
    modes = modes_ref[...].astype(F32).astype(BF16)
    modes = jnp.broadcast_to(modes, (LANES, 2 * n))
    for i in range(2):
        choose = ones_where(iota((n, 2 * n), 1) == 2 * iota((n, 2 * n), 0) + i)
        mode = dot_nt(choose, modes)
        phase = mode * iota((n, LANES), 1).astype(F32)
        phase = phase - lon * jnp.floor(phase * (1.0 / lon))
        real, imag = jnp.cos(phase * (TURN / lon)), jnp.sin(phase * (TURN / lon))
        parts = lon // LANES
        jump = mode - parts * jnp.floor(mode * (1.0 / parts))
        jump_real, jump_imag = jnp.cos(jump * (TURN / parts)), jnp.sin(jump * (TURN / parts))
        for b in range(parts):
            at = pl.ds(b * LANES, LANES)
            table[pl.ds(2 * i * n, n), at] = real.astype(BF16)
            table[pl.ds((2 * i + 1) * n, n), at] = (-imag).astype(BF16)
            real, imag = real * jump_real - imag * jump_imag, imag * jump_real + real * jump_imag
    slot_modes = []
    for i in range(2):
        choose = ones_where(iota((2 * n, n), 0) == 2 * iota((2 * n, n), 1) + i)
        slot_modes += [dot(modes[0:16], choose)] * 2
    scale_v[...] = jnp.where(jnp.concatenate(slot_modes, axis=1) == 0.0, 1.0, 2.0)[0:8]

    def row_major(at):
        j = lax.div(at, n)
        return (at - j * n) * per + j

    regroup = ones_where(iota((group, group), 0) == row_major(iota((1, group), 1)))

    share = pad // PLANE // 2
    own_piece = core * PLANE + spot

    def meet(src, dst, slot, to):
        return pltpu.make_async_remote_copy(
            src,
            dst,
            sum_send.at[slot],
            sum_recv.at[slot],
            device_id=to,
            device_id_type=MESH,
        )

    def meet_rest(buffer, slot):
        count = buffer.shape[0] - 1
        rest = buffer.at[pl.ds(0, count)]
        return meet(rest, rest, slot, {"dp": 1 - core, "wide": me})

    def over_plane(source, target, slot, owners):
        for t in range(PLANE):
            for c in owners:
                at = spot_at(t)
                to = {"dp": c, "wide": line_at[0] + at}

                def go():
                    meet(source(c, at), target.at[own_piece], slot, to).start()

                if t:
                    go()
                else:
                    pl.when(core != c)(go)

    def sum_start(c):
        part[c] = acc[c].reshape(pad // 2, 2, hid)

        @pl.when(core == c)
        def _():
            pieces[own_piece] = part[c, pl.ds(spot * share, share)]

        over_plane(lambda c, s: part.at[c, pl.ds(s * share, share)], pieces, 0, (c,))

    def sum_middle():
        meet_rest(pieces, 0).wait_recv()
        summed = pieces[0]
        for t in range(1, 2 * PLANE):
            summed = summed + pieces[t]
        zpieces[line] = summed
        for t in range(1, lines):
            meet(zpieces.at[line], zpieces.at[line], 1, {"wide": line_at[t] + spot}).start()

    def sum_end():
        meet_rest(zpieces, 1).wait_recv()
        summed = zpieces[0]
        for t in range(1, lines):
            summed = summed + zpieces[t]
        result[own_piece] = summed.astype(BF16)
        over_plane(lambda c, s: result.at[own_piece], result, 2, (0, 1))

    def gather_out(ch):
        for j in range(per):
            row = ch * per + j
            grad = dot_nt(grid_cot[ch, pl.ds(j * pad, pad), :], active[row])
            acc[1] = grad if row == 0 else acc[1] + grad

    def gather_in(ch):
        for j in range(per):
            row = ch * per + j
            grad = dot_nt(columns[row], grad_hidden[j])
            acc[0] = grad if row == 0 else acc[0] + grad

    for ch in range(CHUNKS):
        spread_rest(send1.at[ch], recv1.at[ch], ch).wait_recv()
        arrived = recv1[ch].reshape(group, 4 * pad).T
        arrived = dot(arrived, regroup).astype(BF16)
        for j in range(per):
            for q in range(4):
                lhs[pl.ds(j * pad, pad), pl.ds(q * n, n)] = arrived[
                    q * pad : (q + 1) * pad, j * n : (j + 1) * n
                ]
        grid_cot[ch] = (dot(lhs[...], table[...]) * (1.0 / lon)).astype(BF16)
        last = ch == CHUNKS - 1
        if last:
            gather_out(ch)
            sum_start(1)
        for j in range(per):
            cot_row = grid_cot[ch, pl.ds(j * pad, pad), :]
            back_hidden = dot(wout_t[...], cot_row)
            grad_hidden[j] = (back_hidden * factor[ch * per + j]).astype(BF16)
        if last:
            gather_in(ch)
            sum_start(0)
        for j in range(per):
            dstate[pl.ds(j * pad, pad), :] = dot(win_ext[...], grad_hidden[j]).astype(BF16)
        back = (dot_nt(dstate[...], table[...]) * scale_v[0:1, :]).astype(BF16)
        for j in range(per):
            for q in range(4):
                zbuf[pl.ds(q * pad, pad), pl.ds(j * n, n)] = back[
                    j * pad : (j + 1) * pad, q * n : (q + 1) * n
                ]
        send2[ch] = to_messages(dot_nt(regroup, zbuf[...]).astype(BF16))
        recv2[ch, me] = send2[ch, me]
        spread(send2.at[ch], recv2.at[ch], CHUNKS + ch)
        if last:
            sum_middle()
            sum_end()
        else:
            gather_out(ch)
            gather_in(ch)

    for ch in range(CHUNKS):
        spread_rest(send2.at[ch], recv2.at[ch], CHUNKS + ch).wait_recv()
        arrived = recv2[ch].reshape(group, 4 * pad).T
        for i in range(2):
            got = dot_nt(
                arrived[2 * i * pad : 2 * (i + 1) * pad], legp[i, :, pl.ds(ch * group, group)]
            )
            if ch:
                got = got + out_acc[i]
            if ch < CHUNKS - 1:
                out_acc[i] = got
            else:
                spec_out_v[i] = jnp.concatenate(
                    [got[0:chans], got[pad : pad + chans]], axis=0
                ).astype(BF16)

    spec_out = pltpu.make_async_copy(spec_out_v, spec_grad_ref, load_sem.at[0])
    spec_out.start()
    meet_rest(result, 2).wait_recv()
    sums_out = pltpu.make_async_copy(result, sums_ref, load_sem.at[1])
    sums_out.start()
    for ch in range(CHUNKS):
        spread_rest(send1.at[ch], recv1.at[ch], ch).wait_send()
        spread_rest(send2.at[ch], recv2.at[ch], CHUNKS + ch).wait_send()
    meet_rest(pieces, 0).wait_send()
    meet_rest(zpieces, 1).wait_send()
    meet_rest(result, 2).wait_send()
    sums_out.wait()
    spec_out.wait()


def settle_kernel(
    spec_hbm,
    sums_hbm,
    spec_out,
    gin_out,
    gbias_out,
    gout_out,
    spec_v,
    sums_v,
    gin_v,
    gbias_v,
    gout_v,
    load_sem,
    store_sem,
):
    chans, hid = gin_v.shape
    spec_load = pltpu.make_async_copy(spec_hbm, spec_v, load_sem.at[0])
    sums_load = pltpu.make_async_copy(sums_hbm, sums_v, load_sem.at[1])
    stores = [
        pltpu.make_async_copy(src, dst, store_sem.at[at])
        for at, (src, dst) in enumerate(
            [(spec_v, spec_out), (gin_v, gin_out), (gbias_v, gbias_out), (gout_v, gout_out)]
        )
    ]
    sums_load.start()
    spec_load.start()
    half = sums_v.shape[0] // 2
    pad = half * sums_v.shape[1] * 2
    sums_load.wait()
    grad_in = sums_v[pl.ds(0, half)].astype(F32).reshape(pad, hid)
    gin_v[...] = grad_in[0:chans]
    gbias_v[...] = grad_in[chans : chans + 1]
    stores[1].start()
    stores[2].start()
    gout_v[...] = sums_v[pl.ds(half, half)].astype(F32).reshape(pad, hid)[0:chans]
    stores[3].start()
    spec_load.wait()
    stores[0].start()
    for store in stores:
        store.wait()


def settle(spec_grad, sums, chans, hid):
    anywhere = pl.BlockSpec(memory_space=pl.ANY)
    shapes = [
        jax.ShapeDtypeStruct(spec_grad.shape, spec_grad.dtype),
        jax.ShapeDtypeStruct((chans, hid), F32),
        jax.ShapeDtypeStruct((1, hid), F32),
        jax.ShapeDtypeStruct((chans, hid), F32),
    ]
    held = [spec_grad, sums] + shapes[1:]
    return pl.pallas_call(
        settle_kernel,
        name="settle",
        out_shape=shapes,
        in_specs=[anywhere] * 2,
        out_specs=[anywhere] * 4,
        scratch_shapes=[pltpu.VMEM(x.shape, x.dtype) for x in held]
        + [pltpu.SemaphoreType.DMA((2,)), pltpu.SemaphoreType.DMA((4,))],
        compiler_params=pltpu.CompilerParams(vmem_limit_bytes=56 * 2**20),
    )(spec_grad, sums)


def per_device(
    spec_cot, grid_state, weight_in, bias_in, weight_out, legendre, row_order, mode_order
):
    n = lax.axis_size("wide")
    _, rows, lon, chans = grid_state.shape
    hid = weight_in.shape[1]
    degrees = legendre.shape[1]
    pad = -(-(chans + 3) // 32) * 32
    total, group = rows * n, rows * n // CHUNKS
    per = rows // CHUNKS
    share = pad // PLANE // 2
    message = (CHUNKS, n, per, 4 * pad)
    scratch = [
        pltpu.VMEM((2, 2 * chans, degrees), BF16),
        pltpu.VMEM((2, 2 * chans, degrees), BF16),
        pltpu.VMEM((chans, rows, lon), BF16),
        pltpu.VMEM((chans, hid), BF16),
        pltpu.VMEM((1, hid), F32),
        pltpu.VMEM((chans, hid), BF16),
        pltpu.VMEM((2, degrees, total), BF16),
        pltpu.VMEM((1, total), jnp.int32),
        pltpu.VMEM((1, 2 * n), jnp.int32),
        pltpu.VMEM((2, degrees, total), BF16),
        pltpu.VMEM((2, 2 * pad, degrees), BF16),
        pltpu.VMEM((4 * pad, total), BF16),
        pltpu.VMEM((pad, hid), BF16),
        pltpu.VMEM((hid, pad), BF16),
        pltpu.VMEM((hid, pad), BF16),
        pltpu.VMEM((4 * n, lon), BF16),
        pltpu.VMEM((8, 4 * n), F32),
        pltpu.VMEM((rows, pad, lon), BF16),
        pltpu.VMEM((rows, hid, lon), F32),
        pltpu.VMEM((rows, hid, lon), BF16),
        pltpu.VMEM((per * pad, 4 * n), BF16),
        pltpu.VMEM((CHUNKS, per * pad, lon), BF16),
        pltpu.VMEM((per, hid, lon), BF16),
        pltpu.VMEM((per * pad, lon), BF16),
        pltpu.VMEM((4 * pad, group), BF16),
        pltpu.VMEM((2, 2 * pad, degrees), F32),
        pltpu.VMEM(message, BF16),
        pltpu.VMEM(message, BF16),
        pltpu.VMEM(message, BF16),
        pltpu.VMEM(message, BF16),
        pltpu.VMEM((2, pad, hid), F32),
        pltpu.VMEM((2, pad // 2, 2, hid), F32),
        pltpu.VMEM((2 * PLANE, share, 2, hid), F32),
        pltpu.VMEM((n // PLANE, share, 2, hid), F32),
        pltpu.VMEM((2 * PLANE, share, 2, hid), BF16),
        pltpu.SemaphoreType.DMA((8,)),
        pltpu.SemaphoreType.DMA((2 * CHUNKS,)),
        pltpu.SemaphoreType.DMA((2 * CHUNKS,)),
        pltpu.SemaphoreType.DMA((3,)),
        pltpu.SemaphoreType.DMA((3,)),
        pltpu.SemaphoreType.REGULAR,
    ]
    hbm = pl.BlockSpec(memory_space=pl.ANY)
    spec_grad, sums = pl.pallas_call(
        functools.partial(step_kernel, (n, rows, chans, pad, lon, hid)),
        name="spectral_step",
        out_shape=(
            jax.ShapeDtypeStruct((2, 2 * chans, degrees), BF16),
            jax.ShapeDtypeStruct((2 * PLANE, share, 2, hid), BF16),
        ),
        in_specs=[hbm] * 8,
        out_specs=(hbm, hbm),
        scratch_shapes=scratch,
        compiler_params=pltpu.CompilerParams(
            collective_id=0, has_side_effects=True, vmem_limit_bytes=56 * 2**20
        ),
    )(
        jnp.swapaxes(spec_cot[0], 1, 2),
        jnp.transpose(grid_state[0], (2, 0, 1)),
        weight_in,
        bias_in.reshape(1, hid),
        weight_out.T,
        legendre,
        row_order.reshape(1, total),
        mode_order.reshape(1, 2 * n),
    )
    spec_grad, grad_in, grad_bias, grad_out = settle(spec_grad, sums, chans, hid)
    return (
        jnp.swapaxes(spec_grad, 1, 2)[None],
        grad_in,
        grad_bias.reshape(hid),
        grad_out.T,
    )


def solution(mesh):
    placed = (
        P("dp", "wide", None, None),
        P("dp", "wide", None, None),
        P(),
        P(),
        P(),
        P("wide", None, None),
        P(),
        P(),
    )
    return jax.shard_map(
        per_device,
        mesh=mesh,
        in_specs=placed,
        out_specs=(P("dp", "wide", None, None), P(), P(), P()),
        check_vma=False,
    )
```
